32 devices in a mesh: groups: 2 (over x), dp: 16 (over z, y, core).
Axes of the slice: x: 2, y: 2, z: 4, core: 2. Of those that a mesh axis runs over, the one named last changes fastest.
Arguments:
- activations: bfloat16 [4096, 8192], P(('groups', 'dp')), parts along dimension 0, may hold values from -16 to 16
- out_grads: bfloat16 [4096, 28672], P(('groups', 'dp')), parts along dimension 0, may hold values from -16 to 16
- slot_of_row: int32 [4096], P(('groups', 'dp')), parts along dimension 0, may hold values from -1 to 1023, as said below
- basis_in: bfloat16 [16384, 256], P(('groups', 'dp')), parts along dimension 0, may hold values from -0.0625 to 0.0625
- basis_out: bfloat16 [57344, 256], P(('groups', 'dp')), parts along dimension 0, may hold values from -0.03125 to 0.03125
Outputs:
- corrected: float32 [512, 256], P(('groups', 'dp')), parts along dimension 0
- self_score: float32 [2048], P(('groups', 'dp')), parts along dimension 0
The draws below stay inside these ranges and needn't reach their ends.
There are 2 independent parts, one for each index of `groups`. The reference program is written for one: setup_inputs(seed, part) draws one part's arguments, and reference() takes and returns one part's arrays. A program takes and returns all parts, laid end to end along the dimension named above; each array names one. Nothing has to cross between parts.
Inputs may be any that keep to these rules, and one draw needn't show every extreme that they name: Rows with slot_of_row >= 0 are the valid token rows; every slot 0 to 1023 is named by exactly one row, and slot s belongs to device s // 64 of dp. A device sends at most 8 valid rows to any one device, and some device sends exactly 8 to every device.
All inputs are finite; a program needn't handle non-finite values.
Results may differ from the reference program's by a relative error of at most 0.00056.
Values may be sent and summed in bfloat16 or wider, within the bound.
No kernel may reach another device: no remote copies, remote signals or barrier semaphores. Data moves between devices by JAX's collectives and lax.ppermute only.
A program may use at most 128 MiB of HBM per device.

```python
import math
import jax
import jax.numpy as jnp
from jax import lax

DIN = 8192
DOUT = 28672
ROWS = 128
KS = 256
KA = 256
BAL = 64
N_DP = 16


def draw_slot_of_row(key, part):
    key = jax.random.fold_in(key, 11)
    heavy_key, weight_key, score_key, order_key = jax.random.split(key, 4)
    per_peer = ROWS // N_DP
    heavy = jax.random.randint(heavy_key, (), 0, N_DP)
    weights = jax.random.randint(weight_key, (N_DP,), 1, 9)
    raw_scores = jax.random.randint(score_key, (N_DP, N_DP, per_peer), 0, 65536)
    cell_index = jnp.arange(N_DP * per_peer, dtype=jnp.int32).reshape(N_DP, per_peer)
    scores = raw_scores * weights[None, :, None] * (N_DP * per_peer) + cell_index[None]
    sources = jnp.arange(N_DP, dtype=jnp.int32)
    is_heavy = sources == heavy
    scores = jnp.where(is_heavy[None, :, None], -1, scores).reshape(N_DP, N_DP * per_peer)
    ordering = jnp.argsort(-scores, axis=1)
    ranking = jnp.argsort(ordering, axis=1).reshape(N_DP, N_DP, per_peer)
    chosen = (ranking < BAL - per_peer).astype(jnp.int32)
    per_pair = jnp.where(is_heavy[None, :], per_peer, jnp.sum(chosen, axis=2)).astype(jnp.int32)
    counts = jnp.sum(per_pair, axis=0)
    dest_incl = jnp.cumsum(per_pair, axis=0)
    dest_start = dest_incl - per_pair
    within = jnp.cumsum(per_pair, axis=1) - per_pair
    row_draws = jax.random.randint(order_key, (N_DP, ROWS), 0, 1 << 30)
    position = jnp.argsort(jnp.argsort(row_draws, axis=1), axis=1).astype(jnp.int32)
    dest_of = jnp.sum((dest_incl.T[:, None, :] <= position[:, :, None]).astype(jnp.int32), axis=2)
    dest_safe = jnp.minimum(dest_of, N_DP - 1)
    start_source = jnp.take_along_axis(dest_start.T, dest_safe, axis=1)
    offset = jnp.take_along_axis(within.T, dest_safe, axis=1)
    slots = dest_safe * BAL + offset + position - start_source
    slots = jnp.where(position < counts[:, None], slots, -1)
    return slots.reshape(N_DP * ROWS).astype(jnp.int32)


def draw_out_grads(key, part):
    key = jax.random.fold_in(key, 21)
    row_key, entry_key, common_key = jax.random.split(key, 3)
    common = jax.random.normal(common_key, (1, DOUT), jnp.float32)
    log_scale = jax.random.uniform(row_key, (N_DP * ROWS, 1), jnp.float32, math.log(0.5), math.log(2.0))
    entries = jax.random.normal(entry_key, (N_DP * ROWS, DOUT), jnp.float32)
    mixed = 0.85 * entries + 0.5 * common
    return (jnp.exp(log_scale) * jnp.clip(mixed, -4.0, 4.0)).astype(jnp.bfloat16)


def draw_activations(key, part):
    key = jax.random.fold_in(key, 31)
    row_key, entry_key, common_key = jax.random.split(key, 3)
    common = jax.random.normal(common_key, (1, DIN), jnp.float32)
    log_scale = jax.random.uniform(row_key, (N_DP * ROWS, 1), jnp.float32, math.log(0.5), math.log(2.0))
    entries = jax.random.normal(entry_key, (N_DP * ROWS, DIN), jnp.float32)
    mixed = 0.85 * entries + 0.5 * common
    return (jnp.exp(log_scale) * jnp.clip(mixed, -4.0, 4.0)).astype(jnp.bfloat16)


def block_scale(rng, shape, pieces, low, top_value):
    def one(dim, shards_of):
        draws = jax.random.uniform(jax.random.fold_in(jax.random.fold_in(rng, 6), dim), (shards_of,), jnp.float32, low / len(pieces), top_value / len(pieces))
        return jnp.repeat(jnp.exp(draws), shape[dim] // shards_of).reshape((-1,) + (1,) * (len(shape) - dim - 1))

    factor_of = one(*pieces[0])
    for cut in pieces[1:]:
        factor_of = factor_of * one(*cut)
    return factor_of


def noise(key, shape, deviation, bound, cuts=(), kind=jnp.bfloat16):
    values = deviation * jax.random.normal(key, shape, jnp.float32)
    if cuts:
        values = values * block_scale(key, shape, cuts, -0.22, 0.18)
    return jnp.clip(values, -bound, bound).astype(kind)


def setup_inputs(seed: int = 0, part: int = 0) -> dict:
    splits = jax.random.split(jax.random.key(seed), 6)
    part_keys = jax.random.split(jax.random.fold_in(splits[5], part), 6)
    return {
        "activations": draw_activations(jax.random.fold_in(jax.random.fold_in(splits[5], part), 71), part),
        "out_grads": draw_out_grads(jax.random.fold_in(jax.random.fold_in(splits[5], part), 71), part),
        "slot_of_row": draw_slot_of_row(jax.random.fold_in(jax.random.fold_in(splits[5], part), 71), part),
        "basis_in": noise(part_keys[3], (DIN, KA), DIN ** -0.5, 0.0625, ((0, 16),)),
        "basis_out": noise(part_keys[4], (DOUT, KS), DOUT ** -0.5, 0.03125, ((0, 16),)),
    }


damping = 0.1


def squared_rotation(matrix_rows, basis):
    rotated = jnp.dot(matrix_rows, basis, preferred_element_type=jnp.float32)
    return (rotated * rotated).astype(jnp.bfloat16)


def reference(activations, out_grads, slot_of_row, basis_in, basis_out):
    is_valid = slot_of_row >= 0
    grad_sq = squared_rotation(out_grads, basis_out)
    act_sq = squared_rotation(activations, basis_in)
    grad_masked = jnp.where(is_valid[:, None], grad_sq, jnp.zeros_like(grad_sq))
    corrected = jnp.dot(grad_masked.T, act_sq, preferred_element_type=jnp.float32) / (N_DP * BAL)
    inverse = 1.0 / (corrected + damping)
    weighted = jnp.dot(act_sq.astype(jnp.float32), inverse.T, precision=lax.Precision.HIGHEST)
    scores = jnp.sum(grad_sq.astype(jnp.float32) * weighted, axis=1) / (KS * KA)
    target = jnp.where(is_valid, slot_of_row, N_DP * BAL).astype(jnp.int32)
    self_score = jnp.zeros((N_DP * BAL,), jnp.float32).at[target].set(scores, mode="drop")
    return corrected, self_score
```

```python
import jax
import jax.numpy as jnp
from jax import lax
from jax.sharding import PartitionSpec as P

damping = 0.1


def ring_order(chips):
    if chips == 8:
        return [0, 2, 4, 6, 7, 5, 3, 1]
    return list(range(chips))


def body(activations, out_grads, slot_of_row, basis_in, basis_out):
    devices = lax.axis_size("dp")
    chips = devices // 2
    own_index = lax.axis_index("dp")
    core = own_index % 2
    rows = activations.shape[0]
    balanced = rows // 2
    total_rows = devices * balanced
    out_panel = basis_out.shape[1]
    in_panel = basis_in.shape[1]

    order = ring_order(chips)
    place = [order.index(c) for c in range(chips)]
    position = jnp.array(place, jnp.int32)[own_index // 2]
    order_of = jnp.array(order, jnp.int32)

    def ring(step):
        pairs = []
        for i, chip in enumerate(order):
            to = order[(i + step) % chips]
            pairs += [(2 * chip, 2 * to), (2 * chip + 1, 2 * to + 1)]
        return pairs

    forward, backward = ring(1), ring(-1)
    swap = [(i, i ^ 1) for i in range(devices)]

    def send(x, pairs):
        return lax.ppermute(x, "dp", pairs)

    def owner(distance, which_core):
        return order_of[(position - distance) % chips] * 2 + which_core

    half = chips // 2
    distances = [0]
    for d in range(1, half):
        distances += [d, -d]
    distances += [half]

    def columns(x, depth, distance, which_core):
        start = owner(distance, which_core) * depth
        return lax.dynamic_slice(x, (0, start), (rows, depth))

    def both(x, depth):
        tokens = {}
        for d in distances:
            other = send(columns(x, depth, d, 1 - core), swap)
            tokens[d] = jnp.concatenate([columns(x, depth, d, core), other], axis=0)
        return tokens

    def dot(a, b):
        return jnp.dot(a, b, preferred_element_type=jnp.float32)

    def gather(pieces_of, last_forward, last_backward):
        held = [{0: p} for p in pieces_of]
        for s in range(1, half):
            for h in held:
                h[s] = send(h[s - 1], forward)
                h[-s] = send(h[1 - s], backward)
        for i in last_forward:
            held[i][half] = send(held[i][half - 1], forward)
        for i in last_backward:
            held[i][half] = send(held[i][1 - half], backward)
        return held

    def halves(x):
        h = x.shape[0] // 2
        return [x[:h], x[h:]]

    def project(x, basis):
        depth = basis.shape[0]
        if chips > 8:
            total = dot(x, lax.all_gather(basis, "dp", axis=0, tiled=True))
            return (total * total).astype(jnp.bfloat16)
        tokens = both(x, depth)
        held = gather(halves(basis), [0], [1])
        h = depth // 2
        total = 0.0
        for d in distances:
            total += dot(tokens[d][:, :h], held[0][d]) + dot(tokens[d][:, h:], held[1][d])
        total = total[:rows] + send(total[rows:], swap)
        return (total * total).astype(jnp.bfloat16)

    def everyone(x):
        if chips > 8:
            return lax.all_gather(x, "dp", axis=0, tiled=True)
        held = gather(halves(x), [0], [1])
        mine = jnp.concatenate([h[d] for h in held for d in distances], axis=0)
        return jnp.concatenate([mine, send(mine, swap)], axis=0)

    act_sq = project(activations, basis_in)
    slots = everyone(slot_of_row[:, None])[:, 0]
    all_act = everyone(act_sq)
    grad_sq = project(out_grads, basis_out)
    is_valid = slot_of_row >= 0
    all_grad = everyone(jnp.where(is_valid[:, None], grad_sq, jnp.zeros_like(grad_sq)))

    corrected = (
        lax.dot_general(
            all_grad, all_act, (((0,), (0,)), ((), ())), preferred_element_type=jnp.float32
        )
        / total_rows
    )
    inverse = 1.0 / (corrected + damping)
    wanted = own_index * balanced + jnp.arange(balanced, dtype=jnp.int32)
    pick = (slots[None, :] == wanted[:, None]).astype(jnp.bfloat16)
    own_grad = dot(pick, all_grad)
    own_act = dot(pick, all_act)
    weighted = lax.dot_general(
        own_act, inverse, (((1,), (1,)), ((), ())), precision=lax.Precision.HIGHEST
    )
    self_score = jnp.sum(own_grad * weighted, axis=1) / (out_panel * in_panel)
    panel_rows = out_panel // devices
    own_corrected = lax.dynamic_slice(corrected, (own_index * panel_rows, 0), (panel_rows, in_panel))
    return (own_corrected, self_score)


def solution(mesh):
    return jax.shard_map(
        body,
        mesh=mesh,
        in_specs=(
            P(("groups", "dp"), None),
            P(("groups", "dp"), None),
            P(("groups", "dp")),
            P(("groups", "dp"), None),
            P(("groups", "dp"), None),
        ),
        out_specs=(P(("groups", "dp"), None), P(("groups", "dp"))),
        check_vma=False,
    )
```

```python
import functools

import jax
import jax.numpy as jnp
from jax import lax
from jax.experimental import pallas as pl
from jax.experimental.pallas import tpu as pltpu
from jax.sharding import PartitionSpec as P

damping = 0.1


def ring_order(chips):
    if chips == 8:
        return [0, 2, 4, 6, 7, 5, 3, 1]
    return list(range(chips))


def dot(a, b):
    return jnp.dot(a, b, preferred_element_type=jnp.float32)


def squared(x):
    return (x * x).astype(jnp.bfloat16)


def finish(all_grad, all_act, owners, places, own_index, devices, balanced):
    out_panel, in_panel = all_grad.shape[1], all_act.shape[1]
    masked = jnp.where(owners[:, None] >= 0, all_grad, jnp.zeros_like(all_grad))
    corrected = lax.dot_general(
        masked, all_act, (((0,), (0,)), ((), ())), preferred_element_type=jnp.float32
    ) / (devices * balanced)
    inverse = 1.0 / (corrected + damping)
    wanted = jnp.arange(balanced, dtype=jnp.int32)
    pick = ((owners[None, :] == own_index) & (places[None, :] == wanted[:, None])).astype(jnp.bfloat16)
    own_grad = dot(pick, all_grad)
    own_act = dot(pick, all_act)
    weighted = lax.dot_general(
        own_act, inverse, (((1,), (1,)), ((), ())), precision=lax.Precision.HIGHEST
    )
    self_score = jnp.sum(own_grad * weighted, axis=1) / (out_panel * in_panel)
    panel_rows = out_panel // devices
    own_corrected = lax.dynamic_slice(corrected, (own_index * panel_rows, 0), (panel_rows, in_panel))
    return own_corrected, self_score


def gathered(activations, out_grads, slot_of_row, basis_in, basis_out):
    devices = lax.axis_size("dp")
    own_index = lax.axis_index("dp")
    balanced = activations.shape[0] // 2

    def everyone(x):
        return lax.all_gather(x, "dp", axis=0, tiled=True)

    act_sq = squared(dot(activations, everyone(basis_in)))
    grad_sq = squared(dot(out_grads, everyone(basis_out)))
    slots = everyone(slot_of_row)
    owners = jnp.where(slots >= 0, slots // balanced, -1)
    return finish(
        everyone(grad_sq), everyone(act_sq), owners, slots % balanced, own_index, devices, balanced
    )


def runs(first, count, depth_in, depth_out):
    inside = max(0, min(depth_in - first, count))
    found = []
    if inside:
        found.append((0, first, inside, 0))
    if count > inside:
        found.append((1, first + inside - depth_in, count - inside, inside))
    return found


def project_kernel(parts, depths, owners_ref, act_ref, grad_ref, other_act_ref, other_grad_ref, *refs):
    panels, (mine_ref, theirs_ref, mine_out, theirs_out, block, sems) = (
        refs[: len(parts)],
        refs[len(parts) :],
    )
    rows, width = act_ref.shape[0], panels[0].shape[1]
    sources = ((act_ref, other_act_ref), (grad_ref, other_grad_ref))
    work, at, index = [], 0, 0
    for (slot, first), panel in zip(parts, panels):
        for kind, start, count, within in runs(first, panel.shape[0], *depths):
            column = pl.multiple_of(owners_ref[slot] * depths[kind] + start, 128)
            copies = []
            for j, source in enumerate(sources[kind]):
                copy = pltpu.make_async_copy(
                    source.at[:, pl.ds(column, count)],
                    block.at[pl.ds(j * rows, rows), pl.ds(at, count)],
                    sems.at[index, j],
                )
                copy.start()
                copies.append(copy)
            work.append((kind, at, count, panel.at[pl.ds(within, count), :], copies))
            at += count
            index += 1
    totals = [0.0, 0.0]
    for kind, at, count, panel, copies in work:
        for copy in copies:
            copy.wait()
        totals[kind] += dot(block[:, at : at + count], panel[...])
    for kind, total in enumerate(totals):
        columns = slice(kind * width, (kind + 1) * width)
        mine_out[:, columns] = mine_ref[:, columns] + total[:rows]
        theirs_out[:, columns] = theirs_ref[:, columns] + total[rows:]


def project(owners, tokens, parts, before, depth_in, depth_out):
    rows, width = tokens[0].shape[0], parts[0][2].shape[1]
    panels = [p[2] for p in parts]
    depth = sum(p.shape[0] for p in panels)
    vmem = pl.BlockSpec(memory_space=pltpu.VMEM)
    total = jax.ShapeDtypeStruct((rows, 2 * width), jnp.float32)
    return pl.pallas_call(
        functools.partial(project_kernel, [p[:2] for p in parts], (depth_in, depth_out)),
        out_shape=(total, total),
        in_specs=[pl.BlockSpec(memory_space=pltpu.SMEM)]
        + [pl.BlockSpec(memory_space=pl.ANY)] * 4
        + [vmem] * (len(parts) + 2),
        out_specs=(vmem, vmem),
        scratch_shapes=[
            pltpu.VMEM((2 * rows, depth), tokens[0].dtype),
            pltpu.SemaphoreType.DMA((2 * len(parts), 2)),
        ],
        compiler_params=pltpu.CompilerParams(vmem_limit_bytes=40 * 2**20),
        cost_estimate=pl.CostEstimate(
            flops=4 * rows * depth * width, bytes_accessed=8 * rows * depth, transcendentals=0
        ),
    )(owners, *tokens, *panels, *before)


def last_kernel(scale, rows, me_ref, *refs):
    pieces, (corrected_ref, score_ref, squares, held) = refs[:-4], refs[-4:]
    me = me_ref[0]
    panel_rows, in_panel = corrected_ref.shape
    out_panel = squares.shape[1] - in_panel
    balanced = score_ref.shape[1]
    wanted = lax.broadcasted_iota(jnp.int32, (balanced, rows), 0)
    at, picks = 0, []
    for piece in pieces:
        count = min(piece.shape[0], rows)
        if at % rows:
            count = rows - at % rows
        squares[at : at + count, :] = piece[:count, :]
        at += count
        if at % rows == 0:
            tag = piece[count : count + 16, :][:1].astype(jnp.float32).astype(jnp.int32)
            owner, place = tag[:, :rows], tag[:, rows : 2 * rows]
            picks.append(((owner == me) & (place == wanted)).astype(jnp.float32))
    pick = jnp.concatenate(picks, axis=1).astype(jnp.bfloat16)
    act, grad = squares[:, :in_panel], squares[:, in_panel:]
    corrected = lax.dot_general(
        grad, act, (((0,), (0,)), ((), ())), preferred_element_type=jnp.float32
    ) * scale
    held[...] = corrected
    corrected_ref[...] = held[pl.ds(pl.multiple_of(me * panel_rows, panel_rows), panel_rows), :]
    inverse = 1.0 / (corrected + damping)
    high = inverse.astype(jnp.bfloat16)
    low = (inverse - high.astype(jnp.float32)).astype(jnp.bfloat16)
    own_act = dot(pick, act).astype(jnp.bfloat16)
    own_grad = lax.dot_general(
        grad, pick, (((0,), (1,)), ((), ())), preferred_element_type=jnp.float32
    )
    weighted = sum(
        lax.dot_general(part, own_act, (((1,), (1,)), ((), ())), preferred_element_type=jnp.float32)
        for part in (high, low)
    )
    score_ref[...] = jnp.sum(own_grad * weighted, axis=0, keepdims=True) / (out_panel * in_panel)


def last(me, pieces, rows, out_panel, devices, balanced):
    vmem = pl.BlockSpec(memory_space=pltpu.VMEM)
    width = pieces[0].shape[1]
    in_panel = width - out_panel
    corrected, score = pl.pallas_call(
        functools.partial(last_kernel, 1.0 / (devices * balanced), rows),
        out_shape=(
            jax.ShapeDtypeStruct((out_panel // devices, in_panel), jnp.float32),
            jax.ShapeDtypeStruct((1, balanced), jnp.float32),
        ),
        in_specs=[pl.BlockSpec(memory_space=pltpu.SMEM)] + [vmem] * len(pieces),
        out_specs=(vmem, vmem),
        scratch_shapes=[
            pltpu.VMEM((devices * rows, width), jnp.bfloat16),
            pltpu.VMEM((out_panel, in_panel), jnp.float32),
        ],
        compiler_params=pltpu.CompilerParams(vmem_limit_bytes=40 * 2**20),
    )(me, *pieces)
    return corrected, score.reshape(balanced)


def ringed(activations, out_grads, slot_of_row, basis_in, basis_out):
    devices = lax.axis_size("dp")
    chips = devices // 2
    own_index = lax.axis_index("dp")
    rows = activations.shape[0]
    balanced = rows // 2
    depth_in, width = basis_in.shape
    depth_out = basis_out.shape[0]

    order = ring_order(chips)

    def ring(step):
        pairs = []
        for i, chip in enumerate(order):
            to = order[(i + step) % chips]
            pairs += [(2 * chip, 2 * to), (2 * chip + 1, 2 * to + 1)]
        return pairs

    forward, backward = ring(1), ring(-1)
    swap = [(i, i ^ 1) for i in range(devices)]

    def send(x, pairs):
        return lax.ppermute(x, "dp", pairs)

    half = chips // 2
    distances = [0]
    for d in range(1, half):
        distances += [d, -d]
    distances += [half]

    chip = own_index // 2
    position = jnp.where(chip % 2 == 0, chip // 2, chips - 1 - chip // 2)
    from_position = (position - jnp.array(distances, jnp.int32)) % chips
    owners = jnp.where(
        from_position < half, 2 * from_position, 2 * (chips - 1 - from_position) + 1
    ) * 2 + own_index % 2

    shard = {0: jnp.concatenate([basis_in, basis_out], axis=0)}
    depth = depth_in + depth_out
    cut = depth // 2

    def pieces(d, first, panel):
        return [(distances.index(d), first, panel)]

    def pair(s):
        return send(shard[s - 1], forward), send(shard[1 - s], backward)

    shard[1], shard[-1] = pair(1)
    ready_act, ready_grad, _ = lax.optimization_barrier((activations, out_grads, shard[0]))
    swapped_act, swapped_grad = send(ready_act, swap), send(ready_grad, swap)
    shard[1], shard[-1], swapped_act, swapped_grad = lax.optimization_barrier(
        (shard[1], shard[-1], swapped_act, swapped_grad)
    )
    tokens = (activations, out_grads, swapped_act, swapped_grad)
    totals = [jnp.zeros((rows, 2 * width), jnp.float32)] * 2
    for s in range(1, half):
        parts = pieces(s, 0, shard[s]) + pieces(-s, 0, shard[-s])
        if s == 1:
            parts = pieces(0, 0, shard[0]) + parts
        if s + 1 < half:
            shard[s + 1], shard[-s - 1] = pair(s + 1)
        else:
            upper = send(shard[s][cut:], forward)
            lower = send(shard[-s][:cut], backward)
        totals = project(owners, tokens, parts, totals, depth_in, depth_out)
        if s + 1 < half:
            shard[s + 1], shard[-s - 1], *totals = lax.optimization_barrier(
                (shard[s + 1], shard[-s - 1], *totals)
            )
    parts = pieces(half, cut, upper) + pieces(half, 0, lower)
    mine, theirs = project(owners, tokens, parts, totals, depth_in, depth_out)

    is_valid = slot_of_row >= 0
    owner = jnp.where(is_valid, slot_of_row // balanced, -1)
    tag = jnp.concatenate([owner, slot_of_row % balanced]).astype(jnp.bfloat16)
    tag = jnp.broadcast_to(jnp.pad(tag, (0, 2 * width - 2 * rows))[None, :], (16, 2 * width))
    rotated = mine + send(theirs, swap)
    counts = is_valid[:, None] | (jnp.arange(2 * width) < width)[None, :]
    squares = jnp.where(counts, rotated * rotated, 0.0).astype(jnp.bfloat16)

    held = {0: jnp.concatenate([squares, tag], axis=0)}
    middle = (rows + 16) // 32 * 16
    for s in range(1, half):
        held[s], held[-s] = send(held[s - 1], forward), send(held[1 - s], backward)
    gathered_pieces = [held[d] for d in distances[:-1]]
    gathered_pieces.append(send(held[half - 1][:middle], forward))
    gathered_pieces.append(send(held[1 - half][middle:], backward))
    gathered_pieces += [send(x, swap) for x in gathered_pieces]
    return last(own_index[None], gathered_pieces, rows, width, devices, balanced)


def body(*arrays):
    if lax.axis_size("dp") == 16:
        return ringed(*arrays)
    return gathered(*arrays)


def solution(mesh):
    return jax.shard_map(
        body,
        mesh=mesh,
        in_specs=(
            P(("groups", "dp"), None),
            P(("groups", "dp"), None),
            P(("groups", "dp")),
            P(("groups", "dp"), None),
            P(("groups", "dp"), None),
        ),
        out_specs=(P(("groups", "dp"), None), P(("groups", "dp"))),
        check_vma=False,
    )
```

```python
import functools

import jax
import jax.numpy as jnp
from jax import lax
from jax.experimental import pallas as pl
from jax.experimental.pallas import tpu as pltpu
from jax.sharding import PartitionSpec as P

damping = 0.1


def ring_order(chips):
    if chips == 8:
        return [0, 2, 4, 6, 7, 5, 3, 1]
    return list(range(chips))


def dot(a, b):
    return jnp.dot(a, b, preferred_element_type=jnp.float32)


def squared(x):
    return (x * x).astype(jnp.bfloat16)


def finish(all_grad, all_act, owners, places, own_index, devices, balanced):
    out_panel, in_panel = all_grad.shape[1], all_act.shape[1]
    masked = jnp.where(owners[:, None] >= 0, all_grad, jnp.zeros_like(all_grad))
    corrected = lax.dot_general(
        masked, all_act, (((0,), (0,)), ((), ())), preferred_element_type=jnp.float32
    ) / (devices * balanced)
    inverse = 1.0 / (corrected + damping)
    wanted = jnp.arange(balanced, dtype=jnp.int32)
    pick = ((owners[None, :] == own_index) & (places[None, :] == wanted[:, None])).astype(jnp.bfloat16)
    own_grad = dot(pick, all_grad)
    own_act = dot(pick, all_act)
    weighted = lax.dot_general(
        own_act, inverse, (((1,), (1,)), ((), ())), precision=lax.Precision.HIGHEST
    )
    self_score = jnp.sum(own_grad * weighted, axis=1) / (out_panel * in_panel)
    panel_rows = out_panel // devices
    own_corrected = lax.dynamic_slice(corrected, (own_index * panel_rows, 0), (panel_rows, in_panel))
    return own_corrected, self_score


def gathered(activations, out_grads, slot_of_row, basis_in, basis_out):
    devices = lax.axis_size("dp")
    own_index = lax.axis_index("dp")
    balanced = activations.shape[0] // 2

    def everyone(x):
        return lax.all_gather(x, "dp", axis=0, tiled=True)

    act_sq = squared(dot(activations, everyone(basis_in)))
    grad_sq = squared(dot(out_grads, everyone(basis_out)))
    slots = everyone(slot_of_row)
    owners = jnp.where(slots >= 0, slots // balanced, -1)
    return finish(
        everyone(grad_sq), everyone(act_sq), owners, slots % balanced, own_index, devices, balanced
    )


def runs(first, count, depth_in, depth_out):
    inside = max(0, min(depth_in - first, count))
    found = []
    if inside:
        found.append((0, first, inside, 0))
    if count > inside:
        found.append((1, first + inside - depth_in, count - inside, inside))
    return found


def project_kernel(kinds, parts, depths, owners_ref, *refs):
    sources, refs = refs[: 2 * len(kinds)], refs[2 * len(kinds) :]
    panels, refs = refs[: len(parts)], refs[len(parts) :]
    before, (mine_out, theirs_out, block, sems) = refs[: 2 * len(kinds)], refs[2 * len(kinds) :]
    rows, width = sources[0].shape[0], panels[0].shape[1]
    work, at = [], 0
    for (slot, first), panel in zip(parts, panels):
        for kind, start, count, within in runs(first, panel.shape[0], *depths):
            if kind not in kinds:
                continue
            column = pl.multiple_of(owners_ref[slot] * depths[kind] + start, 128)
            copies = []
            for j in range(2):
                copy = pltpu.make_async_copy(
                    sources[2 * kinds.index(kind) + j].at[:, pl.ds(column, count)],
                    block.at[pl.ds(j * rows, rows), pl.ds(at, count)],
                    sems.at[len(work), j],
                )
                copy.start()
                copies.append(copy)
            work.append((kind, at, count, panel.at[pl.ds(within, count), :], copies))
            at += count
    totals = {}
    for kind, at, count, panel, copies in work:
        for copy in copies:
            copy.wait()
        totals[kind] = totals.get(kind, 0.0) + dot(block[:, at : at + count], panel[...])
    for i, kind in enumerate(kinds):
        columns = slice(i * width, (i + 1) * width)
        mine_out[:, columns] = before[2 * i][...] + totals[kind][:rows]
        theirs_out[:, columns] = before[2 * i + 1][...] + totals[kind][rows:]


def project(owners, kinds, tokens, parts, before, depths):
    sources = [x for kind in kinds for x in tokens[kind]]
    rows, width = sources[0].shape[0], parts[0][2].shape[1]
    panels = [p[2] for p in parts]
    counts = [
        run[2] for p in parts for run in runs(p[1], p[2].shape[0], *depths) if run[0] in kinds
    ]
    vmem = pl.BlockSpec(memory_space=pltpu.VMEM)
    total = jax.ShapeDtypeStruct((rows, len(kinds) * width), jnp.float32)
    return pl.pallas_call(
        functools.partial(project_kernel, kinds, [p[:2] for p in parts], depths),
        out_shape=(total, total),
        in_specs=[pl.BlockSpec(memory_space=pltpu.SMEM)]
        + [pl.BlockSpec(memory_space=pl.ANY)] * len(sources)
        + [vmem] * (len(parts) + len(before)),
        out_specs=(vmem, vmem),
        scratch_shapes=[
            pltpu.VMEM((2 * rows, sum(counts)), sources[0].dtype),
            pltpu.SemaphoreType.DMA((len(counts), 2)),
        ],
        compiler_params=pltpu.CompilerParams(vmem_limit_bytes=16 * 2**20),
        cost_estimate=pl.CostEstimate(flops=1, bytes_accessed=1, transcendentals=0),
    )(
        owners,
        *[pltpu.with_memory_space_constraint(x, pltpu.HBM) for x in sources],
        *[pltpu.with_memory_space_constraint(x, pltpu.VMEM) for x in panels],
        *before,
    )


def last_kernel(scale, rows, me_ref, *refs):
    pieces, (corrected_ref, score_ref, squares, held) = refs[:-4], refs[-4:]
    me = me_ref[0]
    panel_rows, in_panel = corrected_ref.shape
    out_panel = squares.shape[1] - in_panel
    balanced = score_ref.shape[1]
    wanted = lax.broadcasted_iota(jnp.int32, (balanced, rows), 0)
    at, picks = 0, []
    for piece in pieces:
        count = min(piece.shape[0], rows)
        if at % rows:
            count = rows - at % rows
        squares[at : at + count, :] = piece[:count, :]
        at += count
        if at % rows == 0:
            tag = piece[count : count + 16, :][:1].astype(jnp.float32).astype(jnp.int32)
            owner, place = tag[:, :rows], tag[:, rows : 2 * rows]
            picks.append(((owner == me) & (place == wanted)).astype(jnp.float32))
    pick = jnp.concatenate(picks, axis=1).astype(jnp.bfloat16)
    act, grad = squares[:, :in_panel], squares[:, in_panel:]
    corrected = lax.dot_general(
        grad, act, (((0,), (0,)), ((), ())), preferred_element_type=jnp.float32
    ) * scale
    held[...] = corrected
    corrected_ref[...] = held[pl.ds(pl.multiple_of(me * panel_rows, panel_rows), panel_rows), :]
    inverse = 1.0 / (corrected + damping)
    high = inverse.astype(jnp.bfloat16)
    low = (inverse - high.astype(jnp.float32)).astype(jnp.bfloat16)
    own_act = dot(pick, act).astype(jnp.bfloat16)
    own_grad = lax.dot_general(
        grad, pick, (((0,), (1,)), ((), ())), preferred_element_type=jnp.float32
    )
    weighted = sum(
        lax.dot_general(part, own_act, (((1,), (1,)), ((), ())), preferred_element_type=jnp.float32)
        for part in (high, low)
    )
    score_ref[...] = jnp.sum(own_grad * weighted, axis=0, keepdims=True) / (out_panel * in_panel)


def last(me, pieces, rows, out_panel, devices, balanced):
    vmem = pl.BlockSpec(memory_space=pltpu.VMEM)
    width = pieces[0].shape[1]
    in_panel = width - out_panel
    corrected, score = pl.pallas_call(
        functools.partial(last_kernel, 1.0 / (devices * balanced), rows),
        out_shape=(
            jax.ShapeDtypeStruct((out_panel // devices, in_panel), jnp.float32),
            jax.ShapeDtypeStruct((1, balanced), jnp.float32),
        ),
        in_specs=[pl.BlockSpec(memory_space=pltpu.SMEM)] + [vmem] * len(pieces),
        out_specs=(vmem, vmem),
        scratch_shapes=[
            pltpu.VMEM((devices * rows, width), jnp.bfloat16),
            pltpu.VMEM((out_panel, in_panel), jnp.float32),
        ],
        compiler_params=pltpu.CompilerParams(vmem_limit_bytes=16 * 2**20),
    )(me, *pieces)
    return corrected, score.reshape(balanced)


def ringed(activations, out_grads, slot_of_row, basis_in, basis_out):
    devices = lax.axis_size("dp")
    chips = devices // 2
    own_index = lax.axis_index("dp")
    rows = activations.shape[0]
    balanced = rows // 2
    depth_in, width = basis_in.shape
    depth_out = basis_out.shape[0]

    order = ring_order(chips)

    def ring(step):
        pairs = []
        for i, chip in enumerate(order):
            to = order[(i + step) % chips]
            pairs += [(2 * chip, 2 * to), (2 * chip + 1, 2 * to + 1)]
        return pairs

    forward, backward = ring(1), ring(-1)
    swap = [(i, i ^ 1) for i in range(devices)]

    def send(x, pairs):
        return lax.ppermute(x, "dp", pairs)

    half = chips // 2
    distances = [0]
    for d in range(1, half):
        distances += [d, -d]
    distances += [half]

    chip = own_index // 2
    position = jnp.where(chip % 2 == 0, chip // 2, chips - 1 - chip // 2)
    from_position = (position - jnp.array(distances, jnp.int32)) % chips
    owners = jnp.where(
        from_position < half, 2 * from_position, 2 * (chips - 1 - from_position) + 1
    ) * 2 + own_index % 2

    cut = (depth_in + depth_out) // 2
    first = {0: jnp.concatenate([basis_in, basis_out[: cut - depth_in]], axis=0)}
    second = {0: basis_out[cut - depth_in :]}

    def hop(ahead, behind, s):
        ahead[s] = send(ahead[s - 1], forward)
        behind[-s] = send(behind[1 - s], backward)

    def pieces(held, at):
        return [(distances.index(d), 0 if held is first else cut, held[d]) for d in at]

    def add(kinds, parts, totals):
        tokens = [(activations, swapped_act), (out_grads, swapped_grad)]
        return list(project(owners, kinds, tokens, parts, totals, (depth_in, depth_out)))

    def after(held, at, totals):
        got = lax.optimization_barrier(tuple(held[d] for d in at) + tuple(totals))
        for d, x in zip(at, got):
            held[d] = x
        return list(got[len(at) :])

    hop(first, second, 1)
    hop(second, first, 1)
    swapped_grad, swapped_act = send(out_grads, swap), None
    zero = jnp.zeros((rows, width), jnp.float32)
    grad = [zero, zero]
    for s in range(1, half):
        own = pieces(first, [0]) + pieces(second, [0]) if s == 1 else []
        if s + 1 < half:
            hop(first, second, s + 1)
        else:
            first[half], second[half] = send(first[s], forward), send(second[-s], backward)
        grad = add((1,), own + pieces(first, [s]) + pieces(second, [-s]), grad)
        grad = after(second, [s], after(first, [-s], grad))
        if s + 1 < half:
            hop(second, first, s + 1)
        grad = add((1,), pieces(second, [s]) + pieces(first, [-s]), grad)
        if s + 1 < half:
            grad = after(first, [s + 1], after(second, [-s - 1], grad))
    swapped_act = send(activations, swap)
    act = add((0,), pieces(first, distances[:-1]), [zero, zero])
    mine, theirs = add((0, 1), pieces(first, [half]) + pieces(second, [half]), act + grad)

    is_valid = slot_of_row >= 0
    owner = jnp.where(is_valid, slot_of_row // balanced, -1)
    tag = jnp.concatenate([owner, slot_of_row % balanced]).astype(jnp.bfloat16)
    tag = jnp.broadcast_to(jnp.pad(tag, (0, 2 * width - 2 * rows))[None, :], (16, 2 * width))
    rotated = mine + send(theirs, swap)
    counts = is_valid[:, None] | (jnp.arange(2 * width) < width)[None, :]
    squares = jnp.where(counts, rotated * rotated, 0.0).astype(jnp.bfloat16)

    held = {0: jnp.concatenate([squares, tag], axis=0)}
    middle = (rows + 16) // 32 * 16
    for s in range(1, half):
        held[s], held[-s] = send(held[s - 1], forward), send(held[1 - s], backward)
    gathered_pieces = [held[d] for d in distances[:-1]]
    gathered_pieces.append(send(held[half - 1][:middle], forward))
    gathered_pieces.append(send(held[1 - half][middle:], backward))
    gathered_pieces += [send(x, swap) for x in gathered_pieces]
    return last(own_index[None], gathered_pieces, rows, width, devices, balanced)


def body(*arrays):
    if lax.axis_size("dp") == 16:
        return ringed(*arrays)
    return gathered(*arrays)


def solution(mesh):
    return jax.shard_map(
        body,
        mesh=mesh,
        in_specs=(
            P(("groups", "dp"), None),
            P(("groups", "dp"), None),
            P(("groups", "dp")),
            P(("groups", "dp"), None),
            P(("groups", "dp"), None),
        ),
        out_specs=(P(("groups", "dp"), None), P(("groups", "dp"))),
        check_vma=False,
    )
```

```python
import functools

import jax
import jax.numpy as jnp
from jax import lax
from jax.experimental import pallas as pl
from jax.experimental.pallas import tpu as pltpu
from jax.sharding import PartitionSpec as P

damping = 0.1


def ring_order(chips):
    if chips == 8:
        return [0, 2, 4, 6, 7, 5, 3, 1]
    return list(range(chips))


def dot(a, b):
    return jnp.dot(a, b, preferred_element_type=jnp.float32)


def squared(x):
    return (x * x).astype(jnp.bfloat16)


def finish(all_grad, all_act, owners, places, own_index, devices, balanced):
    out_panel, in_panel = all_grad.shape[1], all_act.shape[1]
    masked = jnp.where(owners[:, None] >= 0, all_grad, jnp.zeros_like(all_grad))
    corrected = lax.dot_general(
        masked, all_act, (((0,), (0,)), ((), ())), preferred_element_type=jnp.float32
    ) / (devices * balanced)
    inverse = 1.0 / (corrected + damping)
    wanted = jnp.arange(balanced, dtype=jnp.int32)
    pick = ((owners[None, :] == own_index) & (places[None, :] == wanted[:, None])).astype(jnp.bfloat16)
    own_grad = dot(pick, all_grad)
    own_act = dot(pick, all_act)
    weighted = lax.dot_general(
        own_act, inverse, (((1,), (1,)), ((), ())), precision=lax.Precision.HIGHEST
    )
    self_score = jnp.sum(own_grad * weighted, axis=1) / (out_panel * in_panel)
    panel_rows = out_panel // devices
    own_corrected = lax.dynamic_slice(corrected, (own_index * panel_rows, 0), (panel_rows, in_panel))
    return own_corrected, self_score


def gathered(activations, out_grads, slot_of_row, basis_in, basis_out):
    devices = lax.axis_size("dp")
    own_index = lax.axis_index("dp")
    balanced = activations.shape[0] // 2

    def everyone(x):
        return lax.all_gather(x, "dp", axis=0, tiled=True)

    act_sq = squared(dot(activations, everyone(basis_in)))
    grad_sq = squared(dot(out_grads, everyone(basis_out)))
    slots = everyone(slot_of_row)
    owners = jnp.where(slots >= 0, slots // balanced, -1)
    return finish(
        everyone(grad_sq), everyone(act_sq), owners, slots % balanced, own_index, devices, balanced
    )


def runs(first, count, depth_in, depth_out):
    inside = max(0, min(depth_in - first, count))
    found = []
    if inside:
        found.append((0, first, inside, 0))
    if count > inside:
        found.append((1, first + inside - depth_in, count - inside, inside))
    return found


def project_kernel(kinds, parts, depths, owners_ref, *refs):
    sources, refs = refs[: 2 * len(kinds)], refs[2 * len(kinds) :]
    panels, refs = refs[: len(parts)], refs[len(parts) :]
    before, (mine_out, theirs_out, block, sems) = refs[: 2 * len(kinds)], refs[2 * len(kinds) :]
    rows, width = sources[0].shape[0], panels[0].shape[1]
    work, at = [], 0
    for (slot, first), panel in zip(parts, panels):
        for kind, start, count, within in runs(first, panel.shape[0], *depths):
            if kind not in kinds:
                continue
            column = pl.multiple_of(owners_ref[slot] * depths[kind] + start, 128)
            copies = []
            for j in range(2):
                copy = pltpu.make_async_copy(
                    sources[2 * kinds.index(kind) + j].at[:, pl.ds(column, count)],
                    block.at[pl.ds(j * rows, rows), pl.ds(at, count)],
                    sems.at[len(work), j],
                )
                copy.start()
                copies.append(copy)
            work.append((kind, at, count, panel.at[pl.ds(within, count), :], copies))
            at += count
    totals = {}
    for kind, at, count, panel, copies in work:
        for copy in copies:
            copy.wait()
        totals[kind] = totals.get(kind, 0.0) + dot(block[:, at : at + count], panel[...])
    for i, kind in enumerate(kinds):
        columns = slice(i * width, (i + 1) * width)
        mine_out[:, columns] = before[2 * i][...] + totals[kind][:rows]
        theirs_out[:, columns] = before[2 * i + 1][...] + totals[kind][rows:]


def project(owners, kinds, tokens, parts, before, depths):
    sources = [x for kind in kinds for x in tokens[kind]]
    rows, width = sources[0].shape[0], parts[0][2].shape[1]
    panels = [p[2] for p in parts]
    counts = [
        run[2] for p in parts for run in runs(p[1], p[2].shape[0], *depths) if run[0] in kinds
    ]
    vmem = pl.BlockSpec(memory_space=pltpu.VMEM)
    total = jax.ShapeDtypeStruct((rows, len(kinds) * width), jnp.float32)
    return pl.pallas_call(
        functools.partial(project_kernel, kinds, [p[:2] for p in parts], depths),
        out_shape=(total, total),
        in_specs=[pl.BlockSpec(memory_space=pltpu.SMEM)]
        + [pl.BlockSpec(memory_space=pl.ANY)] * len(sources)
        + [vmem] * (len(parts) + len(before)),
        out_specs=(vmem, vmem),
        scratch_shapes=[
            pltpu.VMEM((2 * rows, sum(counts)), sources[0].dtype),
            pltpu.SemaphoreType.DMA((len(counts), 2)),
        ],
        compiler_params=pltpu.CompilerParams(vmem_limit_bytes=16 * 2**20),
        cost_estimate=pl.CostEstimate(flops=1, bytes_accessed=1, transcendentals=0),
    )(
        owners,
        *[pltpu.with_memory_space_constraint(x, pltpu.HBM) for x in sources],
        *[pltpu.with_memory_space_constraint(x, pltpu.VMEM) for x in panels],
        *before,
    )


def copy_all(copies):
    for copy in copies:
        copy.start()
    for copy in copies:
        copy.wait()


def halves_kernel(upper_ref, lower_ref, first_ref, second_ref, sems):
    above, rest = upper_ref.shape[0], first_ref.shape[0] - upper_ref.shape[0]
    copy_all([
        pltpu.make_async_copy(
            lower_ref.at[pl.ds(rest, second_ref.shape[0]), :], second_ref, sems.at[0]
        ),
        pltpu.make_async_copy(upper_ref, first_ref.at[pl.ds(0, above), :], sems.at[1]),
        pltpu.make_async_copy(
            lower_ref.at[pl.ds(0, rest), :], first_ref.at[pl.ds(above, rest), :], sems.at[2]
        ),
    ])


def halves(upper, lower, cut):
    total, width = upper.shape[0] + lower.shape[0], upper.shape[1]
    vmem = pl.BlockSpec(memory_space=pltpu.VMEM)
    return pl.pallas_call(
        halves_kernel,
        out_shape=(
            jax.ShapeDtypeStruct((cut, width), upper.dtype),
            jax.ShapeDtypeStruct((total - cut, width), upper.dtype),
        ),
        in_specs=[pl.BlockSpec(memory_space=pl.ANY)] * 2,
        out_specs=(vmem, vmem),
        scratch_shapes=[pltpu.SemaphoreType.DMA((3,))],
        compiler_params=pltpu.CompilerParams(vmem_limit_bytes=16 * 2**20),
    )(*[pltpu.with_memory_space_constraint(x, pltpu.HBM) for x in (upper, lower)])


def fetch_kernel(slot, depths, owners_ref, *refs):
    sources, (own_ref, sibling_ref, sems) = refs[:4], refs[4:7]
    copies, at = [], 0
    for kind, depth in enumerate(depths):
        column = pl.multiple_of(owners_ref[slot] * depth, 128)
        for j, block in enumerate((own_ref, sibling_ref)):
            copies.append(
                pltpu.make_async_copy(
                    sources[2 * j + kind].at[:, pl.ds(column, depth)],
                    block.at[:, pl.ds(at, depth)],
                    sems.at[kind, j],
                )
            )
        at += depth
    copy_all(copies)


def fetch(owners, slot, tokens, depth_in, depth_out, after):
    rows = tokens[0].shape[0]
    vmem = pl.BlockSpec(memory_space=pltpu.VMEM)
    block = jax.ShapeDtypeStruct((rows, depth_in + depth_out), tokens[0].dtype)
    got = pl.pallas_call(
        functools.partial(fetch_kernel, slot, (depth_in, depth_out)),
        out_shape=(block, block),
        in_specs=[pl.BlockSpec(memory_space=pltpu.SMEM)] + [pl.BlockSpec(memory_space=pl.ANY)] * 4,
        out_specs=(vmem, vmem),
        scratch_shapes=[pltpu.SemaphoreType.DMA((2, 2))],
        compiler_params=pltpu.CompilerParams(vmem_limit_bytes=16 * 2**20),
        cost_estimate=pl.CostEstimate(flops=1, bytes_accessed=1, transcendentals=0),
    )(owners, *[pltpu.with_memory_space_constraint(x, pltpu.HBM) for x in tokens])
    return [list(got), *after]


def finish_dots_kernel(depth_in, block_ref, first_ref, second_ref, act_ref, grad_ref, out_ref):
    cut, width = first_ref.shape
    out_ref[:, :width] = act_ref[...] + dot(block_ref[:, :depth_in], first_ref[:depth_in, :])
    out_ref[:, width:] = (
        grad_ref[...]
        + dot(block_ref[:, depth_in:cut], first_ref[depth_in:, :])
        + dot(block_ref[:, cut:], second_ref[...])
    )


def finish_dots(block, panels, act, grad, depth_in):
    rows, width = act.shape
    vmem = pl.BlockSpec(memory_space=pltpu.VMEM)
    return pl.pallas_call(
        functools.partial(finish_dots_kernel, depth_in),
        out_shape=jax.ShapeDtypeStruct((rows, 2 * width), jnp.float32),
        in_specs=[vmem] * 5,
        out_specs=vmem,
        compiler_params=pltpu.CompilerParams(vmem_limit_bytes=16 * 2**20),
        cost_estimate=pl.CostEstimate(flops=1, bytes_accessed=1, transcendentals=0),
    )(block, *[pltpu.with_memory_space_constraint(x, pltpu.VMEM) for x in panels], act, grad)


def last_kernel(scale, rows, me_ref, *refs):
    pieces, (corrected_ref, score_ref, squares, held) = refs[:-4], refs[-4:]
    me = me_ref[0]
    panel_rows, in_panel = corrected_ref.shape
    out_panel = squares.shape[1] - in_panel
    balanced = score_ref.shape[1]
    wanted = lax.broadcasted_iota(jnp.int32, (balanced, rows), 0)
    at, picks = 0, []
    for piece in pieces:
        start = 0
        while start < piece.shape[0]:
            count = min(rows - at % rows, piece.shape[0] - start)
            squares[at : at + count, :] = piece[start : start + count, :]
            at, start = at + count, start + count
            if at % rows == 0:
                tag = piece[start : start + 16, :][:1].astype(jnp.float32).astype(jnp.int32)
                owner, place = tag[:, :rows], tag[:, rows : 2 * rows]
                picks.append(((owner == me) & (place == wanted)).astype(jnp.float32))
                start += 16
    pick = jnp.concatenate(picks, axis=1).astype(jnp.bfloat16)
    act, grad = squares[:, :in_panel], squares[:, in_panel:]
    corrected = lax.dot_general(
        grad, act, (((0,), (0,)), ((), ())), preferred_element_type=jnp.float32
    ) * scale
    held[...] = corrected
    corrected_ref[...] = held[pl.ds(pl.multiple_of(me * panel_rows, panel_rows), panel_rows), :]
    inverse = 1.0 / (corrected + damping)
    high = inverse.astype(jnp.bfloat16)
    low = (inverse - high.astype(jnp.float32)).astype(jnp.bfloat16)
    own_act = dot(pick, act).astype(jnp.bfloat16)
    own_grad = lax.dot_general(
        grad, pick, (((0,), (1,)), ((), ())), preferred_element_type=jnp.float32
    )
    weighted = sum(
        lax.dot_general(part, own_act, (((1,), (1,)), ((), ())), preferred_element_type=jnp.float32)
        for part in (high, low)
    )
    score_ref[...] = jnp.sum(own_grad * weighted, axis=0, keepdims=True) / (out_panel * in_panel)


def last(me, pieces, rows, out_panel, devices, balanced):
    vmem = pl.BlockSpec(memory_space=pltpu.VMEM)
    width = pieces[0].shape[1]
    in_panel = width - out_panel
    corrected, score = pl.pallas_call(
        functools.partial(last_kernel, 1.0 / (devices * balanced), rows),
        out_shape=(
            jax.ShapeDtypeStruct((out_panel // devices, in_panel), jnp.float32),
            jax.ShapeDtypeStruct((1, balanced), jnp.float32),
        ),
        in_specs=[pl.BlockSpec(memory_space=pltpu.SMEM)] + [vmem] * len(pieces),
        out_specs=(vmem, vmem),
        scratch_shapes=[
            pltpu.VMEM((devices * rows, width), jnp.bfloat16),
            pltpu.VMEM((out_panel, in_panel), jnp.float32),
        ],
        compiler_params=pltpu.CompilerParams(vmem_limit_bytes=16 * 2**20),
    )(me, *pieces)
    return corrected, score.reshape(balanced)


def ringed(activations, out_grads, slot_of_row, basis_in, basis_out):
    devices = lax.axis_size("dp")
    chips = devices // 2
    own_index = lax.axis_index("dp")
    rows = activations.shape[0]
    balanced = rows // 2
    depth_in, width = basis_in.shape
    depth_out = basis_out.shape[0]

    order = ring_order(chips)

    def ring(step):
        pairs = []
        for i, chip in enumerate(order):
            to = order[(i + step) % chips]
            pairs += [(2 * chip, 2 * to), (2 * chip + 1, 2 * to + 1)]
        return pairs

    forward, backward = ring(1), ring(-1)
    swap = [(i, i ^ 1) for i in range(devices)]

    def send(x, pairs):
        return lax.ppermute(x, "dp", pairs)

    half = chips // 2
    distances = [0]
    for d in range(1, half):
        distances += [d, -d]
    distances += [half]

    chip = own_index // 2
    position = jnp.where(chip % 2 == 0, chip // 2, chips - 1 - chip // 2)
    from_position = (position - jnp.array(distances, jnp.int32)) % chips
    owners = jnp.where(
        from_position < half, 2 * from_position, 2 * (chips - 1 - from_position) + 1
    ) * 2 + own_index % 2

    cut = (depth_in + depth_out) // 2
    first, second = halves(basis_in, basis_out, cut)
    first, second = {0: first}, {0: second}

    def hop(ahead, behind, s):
        ahead[s] = send(ahead[s - 1], forward)
        behind[-s] = send(behind[1 - s], backward)

    def pieces(held, at):
        return [(distances.index(d), 0 if held is first else cut, held[d]) for d in at]

    def add(kinds, parts, totals):
        tokens = [(activations, swapped_act), (out_grads, swapped_grad)]
        return list(project(owners, kinds, tokens, parts, totals, (depth_in, depth_out)))

    def after(held, at, totals):
        got = lax.optimization_barrier(tuple(held[d] for d in at) + tuple(totals))
        for d, x in zip(at, got):
            held[d] = x
        return list(got[len(at) :])

    hop(first, second, 1)
    hop(second, first, 1)
    swapped_grad, swapped_act = send(out_grads, swap), None
    zero = jnp.zeros((rows, width), jnp.float32)
    grad = [zero, zero]
    for s in range(1, half):
        own = pieces(first, [0]) + pieces(second, [0]) if s == 1 else []
        if s + 1 < half:
            hop(first, second, s + 1)
        else:
            first[half], second[half] = send(first[s], forward), send(second[-s], backward)
        grad = add((1,), own + pieces(first, [s]) + pieces(second, [-s]), grad)
        grad = after(second, [s], after(first, [-s], grad))
        if s + 1 < half:
            hop(second, first, s + 1)
        grad = add((1,), pieces(second, [s]) + pieces(first, [-s]), grad)
        if s + 1 < half:
            grad = after(first, [s + 1], after(second, [-s - 1], grad))
    swapped_act = send(activations, swap)
    act = add((0,), pieces(first, distances[:-1]), [zero, zero])
    tokens = (activations, out_grads, swapped_act, swapped_grad)
    block, *act = fetch(owners, chips - 1, tokens, depth_in, depth_out, act)
    panels = (first[half], second[half])
    theirs = finish_dots(block[1], panels, act[1], grad[1], depth_in)
    block[0], swapped = lax.optimization_barrier((block[0], theirs))
    swapped = send(swapped, swap)
    mine = finish_dots(block[0], panels, act[0], grad[0], depth_in)

    is_valid = slot_of_row >= 0
    owner = jnp.where(is_valid, slot_of_row // balanced, -1)
    tag = jnp.concatenate([owner, slot_of_row % balanced]).astype(jnp.bfloat16)
    tag = jnp.broadcast_to(jnp.pad(tag, (0, 2 * width - 2 * rows))[None, :], (16, 2 * width))
    rotated = mine + swapped
    counts = is_valid[:, None] | (jnp.arange(2 * width) < width)[None, :]
    squares = jnp.where(counts, rotated * rotated, 0.0).astype(jnp.bfloat16)

    held = {0: jnp.concatenate([squares, tag], axis=0)}
    for s in range(1, half):
        hop(held, held, s)
    near = jnp.concatenate([held[d] for d in distances[:-3]], axis=0)
    near, held[half - 1], held[1 - half] = lax.optimization_barrier(
        (near, held[half - 1], held[1 - half])
    )
    core = own_index % 2
    farthest = jnp.where(core == 0, held[half - 1], held[1 - half])
    opposite = send(farthest, forward[0::2] + backward[1::2])
    far = jnp.concatenate([held[half - 1], held[1 - half]], axis=0)
    swapped = [send(x, swap) for x in (near, far, opposite)]
    own = [near, far, opposite]
    return last(own_index[None], own + swapped, rows, width, devices, balanced)


def body(*arrays):
    if lax.axis_size("dp") == 16:
        return ringed(*arrays)
    return gathered(*arrays)


def solution(mesh):
    return jax.shard_map(
        body,
        mesh=mesh,
        in_specs=(
            P(("groups", "dp"), None),
            P(("groups", "dp"), None),
            P(("groups", "dp")),
            P(("groups", "dp"), None),
            P(("groups", "dp"), None),
        ),
        out_specs=(P(("groups", "dp"), None), P(("groups", "dp"))),
        check_vma=False,
    )
```

```python
import functools

import jax
import jax.numpy as jnp
from jax import lax
from jax.experimental import pallas as pl
from jax.experimental.pallas import tpu as pltpu
from jax.sharding import PartitionSpec as P

damping = 0.1


def ring_order(chips):
    if chips == 8:
        return [0, 2, 4, 6, 7, 5, 3, 1]
    return list(range(chips))


def dot(a, b):
    return jnp.dot(a, b, preferred_element_type=jnp.float32)


def squared(x):
    return (x * x).astype(jnp.bfloat16)


def finish(all_grad, all_act, owners, places, own_index, devices, balanced):
    out_panel, in_panel = all_grad.shape[1], all_act.shape[1]
    masked = jnp.where(owners[:, None] >= 0, all_grad, jnp.zeros_like(all_grad))
    corrected = lax.dot_general(
        masked, all_act, (((0,), (0,)), ((), ())), preferred_element_type=jnp.float32
    ) / (devices * balanced)
    inverse = 1.0 / (corrected + damping)
    wanted = jnp.arange(balanced, dtype=jnp.int32)
    pick = ((owners[None, :] == own_index) & (places[None, :] == wanted[:, None])).astype(jnp.bfloat16)
    own_grad = dot(pick, all_grad)
    own_act = dot(pick, all_act)
    weighted = lax.dot_general(
        own_act, inverse, (((1,), (1,)), ((), ())), precision=lax.Precision.HIGHEST
    )
    self_score = jnp.sum(own_grad * weighted, axis=1) / (out_panel * in_panel)
    panel_rows = out_panel // devices
    own_corrected = lax.dynamic_slice(corrected, (own_index * panel_rows, 0), (panel_rows, in_panel))
    return own_corrected, self_score


def gathered(activations, out_grads, slot_of_row, basis_in, basis_out):
    devices = lax.axis_size("dp")
    own_index = lax.axis_index("dp")
    balanced = activations.shape[0] // 2

    def everyone(x):
        return lax.all_gather(x, "dp", axis=0, tiled=True)

    act_sq = squared(dot(activations, everyone(basis_in)))
    grad_sq = squared(dot(out_grads, everyone(basis_out)))
    slots = everyone(slot_of_row)
    owners = jnp.where(slots >= 0, slots // balanced, -1)
    return finish(
        everyone(grad_sq), everyone(act_sq), owners, slots % balanced, own_index, devices, balanced
    )


def runs(first, count, depth_in, depth_out):
    inside = max(0, min(depth_in - first, count))
    found = []
    if inside:
        found.append((0, first, inside, 0))
    if count > inside:
        found.append((1, first + inside - depth_in, count - inside, inside))
    return found


def project_kernel(kinds, parts, depths, owners_ref, *refs):
    sources, refs = refs[: 2 * len(kinds)], refs[2 * len(kinds) :]
    panels, refs = refs[: len(parts)], refs[len(parts) :]
    before, (mine_out, theirs_out, block, sems) = refs[: 2 * len(kinds)], refs[2 * len(kinds) :]
    rows, width = sources[0].shape[0], panels[0].shape[1]
    work, at = [], 0
    for (slot, first), panel in zip(parts, panels):
        for kind, start, count, within in runs(first, panel.shape[0], *depths):
            if kind not in kinds:
                continue
            column = pl.multiple_of(owners_ref[slot] * depths[kind] + start, 128)
            copies = []
            for j in range(2):
                copy = pltpu.make_async_copy(
                    sources[2 * kinds.index(kind) + j].at[:, pl.ds(column, count)],
                    block.at[pl.ds(j * rows, rows), pl.ds(at, count)],
                    sems.at[len(work), j],
                )
                copy.start()
                copies.append(copy)
            work.append((kind, at, count, panel.at[pl.ds(within, count), :], copies))
            at += count
    totals = {}
    for kind, at, count, panel, copies in work:
        for copy in copies:
            copy.wait()
        totals[kind] = totals.get(kind, 0.0) + dot(block[:, at : at + count], panel[...])
    for i, kind in enumerate(kinds):
        columns = slice(i * width, (i + 1) * width)
        mine_out[:, columns] = before[2 * i][...] + totals[kind][:rows]
        theirs_out[:, columns] = before[2 * i + 1][...] + totals[kind][rows:]


def project(owners, kinds, tokens, parts, before, depths):
    sources = [x for kind in kinds for x in tokens[kind]]
    rows, width = sources[0].shape[0], parts[0][2].shape[1]
    panels = [p[2] for p in parts]
    counts = [
        run[2] for p in parts for run in runs(p[1], p[2].shape[0], *depths) if run[0] in kinds
    ]
    vmem = pl.BlockSpec(memory_space=pltpu.VMEM)
    total = jax.ShapeDtypeStruct((rows, len(kinds) * width), jnp.float32)
    return pl.pallas_call(
        functools.partial(project_kernel, kinds, [p[:2] for p in parts], depths),
        out_shape=(total, total),
        in_specs=[pl.BlockSpec(memory_space=pltpu.SMEM)]
        + [pl.BlockSpec(memory_space=pl.ANY)] * len(sources)
        + [vmem] * (len(parts) + len(before)),
        out_specs=(vmem, vmem),
        scratch_shapes=[
            pltpu.VMEM((2 * rows, sum(counts)), sources[0].dtype),
            pltpu.SemaphoreType.DMA((len(counts), 2)),
        ],
        compiler_params=pltpu.CompilerParams(vmem_limit_bytes=16 * 2**20),
        cost_estimate=pl.CostEstimate(flops=1, bytes_accessed=1, transcendentals=0),
    )(
        owners,
        *[pltpu.with_memory_space_constraint(x, pltpu.HBM) for x in sources],
        *[pltpu.with_memory_space_constraint(x, pltpu.VMEM) for x in panels],
        *before,
    )


def copy_all(copies):
    for copy in copies:
        copy.start()
    for copy in copies:
        copy.wait()


def halves_kernel(upper_ref, lower_ref, first_ref, second_ref, sems):
    above, rest = upper_ref.shape[0], first_ref.shape[0] - upper_ref.shape[0]
    copy_all([
        pltpu.make_async_copy(
            lower_ref.at[pl.ds(rest, second_ref.shape[0]), :], second_ref, sems.at[0]
        ),
        pltpu.make_async_copy(upper_ref, first_ref.at[pl.ds(0, above), :], sems.at[1]),
        pltpu.make_async_copy(
            lower_ref.at[pl.ds(0, rest), :], first_ref.at[pl.ds(above, rest), :], sems.at[2]
        ),
    ])


def halves(upper, lower, cut):
    total, width = upper.shape[0] + lower.shape[0], upper.shape[1]
    vmem = pl.BlockSpec(memory_space=pltpu.VMEM)
    return pl.pallas_call(
        halves_kernel,
        out_shape=(
            jax.ShapeDtypeStruct((cut, width), upper.dtype),
            jax.ShapeDtypeStruct((total - cut, width), upper.dtype),
        ),
        in_specs=[pl.BlockSpec(memory_space=pl.ANY)] * 2,
        out_specs=(vmem, vmem),
        scratch_shapes=[pltpu.SemaphoreType.DMA((3,))],
        compiler_params=pltpu.CompilerParams(vmem_limit_bytes=16 * 2**20),
    )(*[pltpu.with_memory_space_constraint(x, pltpu.HBM) for x in (upper, lower)])


def fetch_kernel(slot, depths, owners_ref, *refs):
    sources, (own_ref, sibling_ref, sems) = refs[:4], refs[4:7]
    copies, at = [], 0
    for kind, depth in enumerate(depths):
        column = pl.multiple_of(owners_ref[slot] * depth, 128)
        for j, block in enumerate((own_ref, sibling_ref)):
            copies.append(
                pltpu.make_async_copy(
                    sources[2 * j + kind].at[:, pl.ds(column, depth)],
                    block.at[:, pl.ds(at, depth)],
                    sems.at[kind, j],
                )
            )
        at += depth
    copy_all(copies)


def fetch(owners, slot, tokens, depth_in, depth_out, after):
    rows = tokens[0].shape[0]
    vmem = pl.BlockSpec(memory_space=pltpu.VMEM)
    block = jax.ShapeDtypeStruct((rows, depth_in + depth_out), tokens[0].dtype)
    got = pl.pallas_call(
        functools.partial(fetch_kernel, slot, (depth_in, depth_out)),
        out_shape=(block, block),
        in_specs=[pl.BlockSpec(memory_space=pltpu.SMEM)] + [pl.BlockSpec(memory_space=pl.ANY)] * 4,
        out_specs=(vmem, vmem),
        scratch_shapes=[pltpu.SemaphoreType.DMA((2, 2))],
        compiler_params=pltpu.CompilerParams(vmem_limit_bytes=16 * 2**20),
        cost_estimate=pl.CostEstimate(flops=1, bytes_accessed=1, transcendentals=0),
    )(owners, *[pltpu.with_memory_space_constraint(x, pltpu.HBM) for x in tokens])
    return [list(got), *after]


def finish_dots_kernel(depth_in, block_ref, first_ref, second_ref, act_ref, grad_ref, out_ref):
    cut, width = first_ref.shape
    out_ref[:, :width] = act_ref[...] + dot(block_ref[:, :depth_in], first_ref[:depth_in, :])
    out_ref[:, width:] = (
        grad_ref[...]
        + dot(block_ref[:, depth_in:cut], first_ref[depth_in:, :])
        + dot(block_ref[:, cut:], second_ref[...])
    )


def finish_dots(block, panels, act, grad, depth_in):
    rows, width = act.shape
    vmem = pl.BlockSpec(memory_space=pltpu.VMEM)
    return pl.pallas_call(
        functools.partial(finish_dots_kernel, depth_in),
        out_shape=jax.ShapeDtypeStruct((rows, 2 * width), jnp.float32),
        in_specs=[vmem] * 5,
        out_specs=vmem,
        compiler_params=pltpu.CompilerParams(vmem_limit_bytes=16 * 2**20),
        cost_estimate=pl.CostEstimate(flops=1, bytes_accessed=1, transcendentals=0),
    )(block, *[pltpu.with_memory_space_constraint(x, pltpu.VMEM) for x in panels], act, grad)


def last_kernel(scale, rows, me_ref, *refs):
    pieces, (corrected_ref, score_ref, squares, held) = refs[:-4], refs[-4:]
    me = me_ref[0]
    panel_rows, in_panel = corrected_ref.shape
    out_panel = squares.shape[1] - in_panel
    balanced = score_ref.shape[1]
    wanted = lax.broadcasted_iota(jnp.int32, (balanced, rows), 0)
    at, picks = 0, []
    for piece in pieces:
        start = 0
        while start < piece.shape[0]:
            count = min(rows - at % rows, piece.shape[0] - start)
            squares[at : at + count, :] = piece[start : start + count, :]
            at, start = at + count, start + count
            if at % rows == 0:
                tag = piece[start : start + 16, :][:1].astype(jnp.float32).astype(jnp.int32)
                owner, place = tag[:, :rows], tag[:, rows : 2 * rows]
                picks.append(((owner == me) & (place == wanted)).astype(jnp.float32))
                start += 16
    pick = jnp.concatenate(picks, axis=1).astype(jnp.bfloat16)
    act, grad = squares[:, :in_panel], squares[:, in_panel:]
    corrected = lax.dot_general(
        grad, act, (((0,), (0,)), ((), ())), preferred_element_type=jnp.float32
    ) * scale
    held[...] = corrected
    corrected_ref[...] = held[pl.ds(pl.multiple_of(me * panel_rows, panel_rows), panel_rows), :]
    inverse = 1.0 / (corrected + damping)
    high = inverse.astype(jnp.bfloat16)
    low = (inverse - high.astype(jnp.float32)).astype(jnp.bfloat16)
    own_act = dot(pick, act).astype(jnp.bfloat16)
    own_grad = lax.dot_general(
        grad, pick, (((0,), (1,)), ((), ())), preferred_element_type=jnp.float32
    )
    weighted = sum(
        lax.dot_general(part, own_act, (((1,), (1,)), ((), ())), preferred_element_type=jnp.float32)
        for part in (high, low)
    )
    score_ref[...] = jnp.sum(own_grad * weighted, axis=0, keepdims=True) / (out_panel * in_panel)


def last(me, pieces, rows, out_panel, devices, balanced):
    vmem = pl.BlockSpec(memory_space=pltpu.VMEM)
    width = pieces[0].shape[1]
    in_panel = width - out_panel
    corrected, score = pl.pallas_call(
        functools.partial(last_kernel, 1.0 / (devices * balanced), rows),
        out_shape=(
            jax.ShapeDtypeStruct((out_panel // devices, in_panel), jnp.float32),
            jax.ShapeDtypeStruct((1, balanced), jnp.float32),
        ),
        in_specs=[pl.BlockSpec(memory_space=pltpu.SMEM)] + [vmem] * len(pieces),
        out_specs=(vmem, vmem),
        scratch_shapes=[
            pltpu.VMEM((devices * rows, width), jnp.bfloat16),
            pltpu.VMEM((out_panel, in_panel), jnp.float32),
        ],
        compiler_params=pltpu.CompilerParams(vmem_limit_bytes=16 * 2**20),
    )(me, *pieces)
    return corrected, score.reshape(balanced)


def ringed(activations, out_grads, slot_of_row, basis_in, basis_out):
    devices = lax.axis_size("dp")
    chips = devices // 2
    own_index = lax.axis_index("dp")
    rows = activations.shape[0]
    balanced = rows // 2
    depth_in, width = basis_in.shape
    depth_out = basis_out.shape[0]

    order = ring_order(chips)

    def ring(step):
        pairs = []
        for i, chip in enumerate(order):
            to = order[(i + step) % chips]
            pairs += [(2 * chip, 2 * to), (2 * chip + 1, 2 * to + 1)]
        return pairs

    forward, backward = ring(1), ring(-1)
    swap = [(i, i ^ 1) for i in range(devices)]

    def send(x, pairs):
        return lax.ppermute(x, "dp", pairs)

    half = chips // 2
    distances = [0]
    for d in range(1, half):
        distances += [d, -d]
    distances += [half]

    chip = own_index // 2
    position = jnp.where(chip % 2 == 0, chip // 2, chips - 1 - chip // 2)
    from_position = (position - jnp.array(distances, jnp.int32)) % chips
    owners = jnp.where(
        from_position < half, 2 * from_position, 2 * (chips - 1 - from_position) + 1
    ) * 2 + own_index % 2

    cut = (depth_in + depth_out) // 2
    first, second = halves(basis_in, basis_out, cut)
    first, second = {0: first}, {0: second}

    def hop(ahead, behind, s):
        ahead[s] = send(ahead[s - 1], forward)
        behind[-s] = send(behind[1 - s], backward)

    def pieces(held, at):
        return [(distances.index(d), 0 if held is first else cut, held[d]) for d in at]

    def add(kinds, parts, totals):
        tokens = [(activations, swapped_act), (out_grads, swapped_grad)]
        return list(project(owners, kinds, tokens, parts, totals, (depth_in, depth_out)))

    def after(held, at, totals):
        got = lax.optimization_barrier(tuple(held[d] for d in at) + tuple(totals))
        for d, x in zip(at, got):
            held[d] = x
        return list(got[len(at) :])

    swapped_act, swapped_grad = send(activations, swap), send(out_grads, swap)
    hop(first, second, 1)
    second[1] = send(second[0], forward)
    ready, swapped_act = lax.optimization_barrier((first[0], swapped_act))
    first[-1] = send(ready, backward)
    zero = jnp.zeros((rows, width), jnp.float32)
    grad = [zero, zero]
    for s in range(1, half):
        own = pieces(first, [0]) + pieces(second, [0]) if s == 1 else []
        if s + 1 < half:
            hop(first, second, s + 1)
        else:
            first[half], second[half] = send(first[s], forward), send(second[-s], backward)
        grad = add((1,), own + pieces(first, [s]) + pieces(second, [-s]), grad)
        grad = after(second, [s], after(first, [-s], grad))
        if s + 1 < half:
            hop(second, first, s + 1)
        grad = add((1,), pieces(second, [s]) + pieces(first, [-s]), grad)
        if s + 1 < half:
            grad = after(first, [s + 1], after(second, [-s - 1], grad))
    act = add((0,), pieces(first, distances[:-1]), [zero, zero])
    tokens = (activations, out_grads, swapped_act, swapped_grad)
    block, *act = fetch(owners, chips - 1, tokens, depth_in, depth_out, act)
    panels = (first[half], second[half])
    theirs = finish_dots(block[1], panels, act[1], grad[1], depth_in)
    block[0], swapped = lax.optimization_barrier((block[0], theirs))
    swapped = send(swapped, swap)
    mine = finish_dots(block[0], panels, act[0], grad[0], depth_in)

    is_valid = slot_of_row >= 0
    owner = jnp.where(is_valid, slot_of_row // balanced, -1)
    tag = jnp.concatenate([owner, slot_of_row % balanced]).astype(jnp.bfloat16)
    tag = jnp.broadcast_to(jnp.pad(tag, (0, 2 * width - 2 * rows))[None, :], (16, 2 * width))
    rotated = mine + swapped
    counts = is_valid[:, None] | (jnp.arange(2 * width) < width)[None, :]
    squares = jnp.where(counts, rotated * rotated, 0.0).astype(jnp.bfloat16)

    held = {0: jnp.concatenate([squares, tag], axis=0)}
    for s in range(1, half):
        hop(held, held, s)
    near = jnp.concatenate([held[d] for d in distances[:-3]], axis=0)
    near, held[half - 1], held[1 - half] = lax.optimization_barrier(
        (near, held[half - 1], held[1 - half])
    )
    core = own_index % 2
    farthest = jnp.where(core == 0, held[half - 1], held[1 - half])
    opposite = send(farthest, forward[0::2] + backward[1::2])
    far = jnp.concatenate([held[half - 1], held[1 - half]], axis=0)
    swapped = [send(x, swap) for x in (near, far, opposite)]
    own = [near, far, opposite]
    return last(own_index[None], own + swapped, rows, width, devices, balanced)


def body(*arrays):
    if lax.axis_size("dp") == 16:
        return ringed(*arrays)
    return gathered(*arrays)


def solution(mesh):
    return jax.shard_map(
        body,
        mesh=mesh,
        in_specs=(
            P(("groups", "dp"), None),
            P(("groups", "dp"), None),
            P(("groups", "dp")),
            P(("groups", "dp"), None),
            P(("groups", "dp"), None),
        ),
        out_specs=(P(("groups", "dp"), None), P(("groups", "dp"))),
        check_vma=False,
    )
```

```python
import functools

import jax
import jax.numpy as jnp
from jax import lax
from jax.experimental import pallas as pl
from jax.experimental.pallas import tpu as pltpu
from jax.sharding import PartitionSpec as P

damping = 0.1


def ring_order(chips):
    if chips == 8:
        return [0, 2, 4, 6, 7, 5, 3, 1]
    return list(range(chips))


def dot(a, b):
    return jnp.dot(a, b, preferred_element_type=jnp.float32)


def squared(x):
    return (x * x).astype(jnp.bfloat16)


def finish(all_grad, all_act, owners, places, own_index, devices, balanced):
    out_panel, in_panel = all_grad.shape[1], all_act.shape[1]
    masked = jnp.where(owners[:, None] >= 0, all_grad, jnp.zeros_like(all_grad))
    corrected = lax.dot_general(
        masked, all_act, (((0,), (0,)), ((), ())), preferred_element_type=jnp.float32
    ) / (devices * balanced)
    inverse = 1.0 / (corrected + damping)
    wanted = jnp.arange(balanced, dtype=jnp.int32)
    pick = ((owners[None, :] == own_index) & (places[None, :] == wanted[:, None])).astype(jnp.bfloat16)
    own_grad = dot(pick, all_grad)
    own_act = dot(pick, all_act)
    weighted = lax.dot_general(
        own_act, inverse, (((1,), (1,)), ((), ())), precision=lax.Precision.HIGHEST
    )
    self_score = jnp.sum(own_grad * weighted, axis=1) / (out_panel * in_panel)
    panel_rows = out_panel // devices
    own_corrected = lax.dynamic_slice(corrected, (own_index * panel_rows, 0), (panel_rows, in_panel))
    return own_corrected, self_score


def gathered(activations, out_grads, slot_of_row, basis_in, basis_out):
    devices = lax.axis_size("dp")
    own_index = lax.axis_index("dp")
    balanced = activations.shape[0] // 2

    def everyone(x):
        return lax.all_gather(x, "dp", axis=0, tiled=True)

    act_sq = squared(dot(activations, everyone(basis_in)))
    grad_sq = squared(dot(out_grads, everyone(basis_out)))
    slots = everyone(slot_of_row)
    owners = jnp.where(slots >= 0, slots // balanced, -1)
    return finish(
        everyone(grad_sq), everyone(act_sq), owners, slots % balanced, own_index, devices, balanced
    )


def runs(first, count, depth_in, depth_out):
    inside = max(0, min(depth_in - first, count))
    found = []
    if inside:
        found.append((0, first, inside, 0))
    if count > inside:
        found.append((1, first + inside - depth_in, count - inside, inside))
    return found


def project_kernel(kinds, parts, depths, owners_ref, *refs):
    sources, refs = refs[: 2 * len(kinds)], refs[2 * len(kinds) :]
    panels, refs = refs[: len(parts)], refs[len(parts) :]
    before, (mine_out, theirs_out, block, sems) = refs[: 2 * len(kinds)], refs[2 * len(kinds) :]
    rows, width = sources[0].shape[0], panels[0].shape[1]
    work, at = [], 0
    for (slot, first), panel in zip(parts, panels):
        for kind, start, count, within in runs(first, panel.shape[0], *depths):
            if kind not in kinds:
                continue
            column = pl.multiple_of(owners_ref[slot] * depths[kind] + start, 128)
            copies = []
            for j in range(2):
                copy = pltpu.make_async_copy(
                    sources[2 * kinds.index(kind) + j].at[:, pl.ds(column, count)],
                    block.at[pl.ds(j * rows, rows), pl.ds(at, count)],
                    sems.at[len(work), j],
                )
                copy.start()
                copies.append(copy)
            work.append((kind, at, count, panel.at[pl.ds(within, count), :], copies))
            at += count
    totals = {}
    for kind, at, count, panel, copies in work:
        for copy in copies:
            copy.wait()
        totals[kind] = totals.get(kind, 0.0) + dot(block[:, at : at + count], panel[...])
    for i, kind in enumerate(kinds):
        columns = slice(i * width, (i + 1) * width)
        mine_out[:, columns] = before[2 * i][...] + totals[kind][:rows]
        theirs_out[:, columns] = before[2 * i + 1][...] + totals[kind][rows:]


def project(owners, kinds, tokens, parts, before, depths):
    sources = [x for kind in kinds for x in tokens[kind]]
    rows, width = sources[0].shape[0], parts[0][2].shape[1]
    panels = [p[2] for p in parts]
    counts = [
        run[2] for p in parts for run in runs(p[1], p[2].shape[0], *depths) if run[0] in kinds
    ]
    vmem = pl.BlockSpec(memory_space=pltpu.VMEM)
    total = jax.ShapeDtypeStruct((rows, len(kinds) * width), jnp.float32)
    return pl.pallas_call(
        functools.partial(project_kernel, kinds, [p[:2] for p in parts], depths),
        out_shape=(total, total),
        in_specs=[pl.BlockSpec(memory_space=pltpu.SMEM)]
        + [pl.BlockSpec(memory_space=pl.ANY)] * len(sources)
        + [vmem] * (len(parts) + len(before)),
        out_specs=(vmem, vmem),
        scratch_shapes=[
            pltpu.VMEM((2 * rows, sum(counts)), sources[0].dtype),
            pltpu.SemaphoreType.DMA((len(counts), 2)),
        ],
        compiler_params=pltpu.CompilerParams(vmem_limit_bytes=16 * 2**20),
        cost_estimate=pl.CostEstimate(flops=1, bytes_accessed=1, transcendentals=0),
    )(
        owners,
        *[pltpu.with_memory_space_constraint(x, pltpu.HBM) for x in sources],
        *[pltpu.with_memory_space_constraint(x, pltpu.VMEM) for x in panels],
        *before,
    )


def copy_all(copies):
    for copy in copies:
        copy.start()
    for copy in copies:
        copy.wait()


def halves_kernel(upper_ref, lower_ref, first_ref, second_ref, sems):
    above, rest = upper_ref.shape[0], first_ref.shape[0] - upper_ref.shape[0]
    copy_all([
        pltpu.make_async_copy(
            lower_ref.at[pl.ds(rest, second_ref.shape[0]), :], second_ref, sems.at[0]
        ),
        pltpu.make_async_copy(upper_ref, first_ref.at[pl.ds(0, above), :], sems.at[1]),
        pltpu.make_async_copy(
            lower_ref.at[pl.ds(0, rest), :], first_ref.at[pl.ds(above, rest), :], sems.at[2]
        ),
    ])


def halves(upper, lower, cut):
    total, width = upper.shape[0] + lower.shape[0], upper.shape[1]
    vmem = pl.BlockSpec(memory_space=pltpu.VMEM)
    return pl.pallas_call(
        halves_kernel,
        out_shape=(
            jax.ShapeDtypeStruct((cut, width), upper.dtype),
            jax.ShapeDtypeStruct((total - cut, width), upper.dtype),
        ),
        in_specs=[pl.BlockSpec(memory_space=pl.ANY)] * 2,
        out_specs=(vmem, vmem),
        scratch_shapes=[pltpu.SemaphoreType.DMA((3,))],
        compiler_params=pltpu.CompilerParams(vmem_limit_bytes=16 * 2**20),
    )(*[pltpu.with_memory_space_constraint(x, pltpu.HBM) for x in (upper, lower)])


def fetch_kernel(slot, depths, owners_ref, *refs):
    sources, (own_ref, sibling_ref, sems) = refs[:4], refs[4:7]
    copies, at = [], 0
    for kind, depth in enumerate(depths):
        column = pl.multiple_of(owners_ref[slot] * depth, 128)
        for j, block in enumerate((own_ref, sibling_ref)):
            copies.append(
                pltpu.make_async_copy(
                    sources[2 * j + kind].at[:, pl.ds(column, depth)],
                    block.at[:, pl.ds(at, depth)],
                    sems.at[kind, j],
                )
            )
        at += depth
    copy_all(copies)


def fetch(owners, slot, tokens, depth_in, depth_out, after):
    rows = tokens[0].shape[0]
    vmem = pl.BlockSpec(memory_space=pltpu.VMEM)
    block = jax.ShapeDtypeStruct((rows, depth_in + depth_out), tokens[0].dtype)
    got = pl.pallas_call(
        functools.partial(fetch_kernel, slot, (depth_in, depth_out)),
        out_shape=(block, block),
        in_specs=[pl.BlockSpec(memory_space=pltpu.SMEM)] + [pl.BlockSpec(memory_space=pl.ANY)] * 4,
        out_specs=(vmem, vmem),
        scratch_shapes=[pltpu.SemaphoreType.DMA((2, 2))],
        compiler_params=pltpu.CompilerParams(vmem_limit_bytes=16 * 2**20),
        cost_estimate=pl.CostEstimate(flops=1, bytes_accessed=1, transcendentals=0),
    )(owners, *[pltpu.with_memory_space_constraint(x, pltpu.HBM) for x in tokens])
    return [list(got), *after]


def finish_dots_kernel(depth_in, block_ref, first_ref, second_ref, act_ref, grad_ref, out_ref):
    cut, width = first_ref.shape
    out_ref[:, :width] = act_ref[...] + dot(block_ref[:, :depth_in], first_ref[:depth_in, :])
    out_ref[:, width:] = (
        grad_ref[...]
        + dot(block_ref[:, depth_in:cut], first_ref[depth_in:, :])
        + dot(block_ref[:, cut:], second_ref[...])
    )


def finish_dots(block, panels, act, grad, depth_in):
    rows, width = act.shape
    vmem = pl.BlockSpec(memory_space=pltpu.VMEM)
    return pl.pallas_call(
        functools.partial(finish_dots_kernel, depth_in),
        out_shape=jax.ShapeDtypeStruct((rows, 2 * width), jnp.float32),
        in_specs=[vmem] * 5,
        out_specs=vmem,
        compiler_params=pltpu.CompilerParams(vmem_limit_bytes=16 * 2**20),
        cost_estimate=pl.CostEstimate(flops=1, bytes_accessed=1, transcendentals=0),
    )(block, *[pltpu.with_memory_space_constraint(x, pltpu.VMEM) for x in panels], act, grad)


def last_kernel(scale, rows, me_ref, *refs):
    pieces, (corrected_ref, score_ref, squares, held) = refs[:-4], refs[-4:]
    me = me_ref[0]
    panel_rows, in_panel = corrected_ref.shape
    out_panel = squares.shape[1] - in_panel
    balanced = score_ref.shape[1]
    wanted = lax.broadcasted_iota(jnp.int32, (balanced, rows), 0)
    at, picks = 0, []
    for piece in pieces:
        start = 0
        while start < piece.shape[0]:
            count = min(rows - at % rows, piece.shape[0] - start)
            squares[at : at + count, :] = piece[start : start + count, :]
            at, start = at + count, start + count
            if at % rows == 0:
                tag = piece[start : start + 16, :][:1].astype(jnp.float32).astype(jnp.int32)
                owner, place = tag[:, :rows], tag[:, rows : 2 * rows]
                picks.append(((owner == me) & (place == wanted)).astype(jnp.float32))
                start += 16
    pick = jnp.concatenate(picks, axis=1).astype(jnp.bfloat16)
    act, grad = squares[:, :in_panel], squares[:, in_panel:]
    corrected = lax.dot_general(
        grad, act, (((0,), (0,)), ((), ())), preferred_element_type=jnp.float32
    ) * scale
    held[...] = corrected
    corrected_ref[...] = held[pl.ds(pl.multiple_of(me * panel_rows, panel_rows), panel_rows), :]
    inverse = 1.0 / (corrected + damping)
    high = inverse.astype(jnp.bfloat16)
    low = (inverse - high.astype(jnp.float32)).astype(jnp.bfloat16)
    own_act = dot(pick, act).astype(jnp.bfloat16)
    own_grad = lax.dot_general(
        grad, pick, (((0,), (1,)), ((), ())), preferred_element_type=jnp.float32
    )
    weighted = sum(
        lax.dot_general(part, own_act, (((1,), (1,)), ((), ())), preferred_element_type=jnp.float32)
        for part in (high, low)
    )
    score_ref[...] = jnp.sum(own_grad * weighted, axis=0, keepdims=True) / (out_panel * in_panel)


def last(me, pieces, rows, out_panel, devices, balanced):
    vmem = pl.BlockSpec(memory_space=pltpu.VMEM)
    width = pieces[0].shape[1]
    in_panel = width - out_panel
    corrected, score = pl.pallas_call(
        functools.partial(last_kernel, 1.0 / (devices * balanced), rows),
        out_shape=(
            jax.ShapeDtypeStruct((out_panel // devices, in_panel), jnp.float32),
            jax.ShapeDtypeStruct((1, balanced), jnp.float32),
        ),
        in_specs=[pl.BlockSpec(memory_space=pltpu.SMEM)] + [vmem] * len(pieces),
        out_specs=(vmem, vmem),
        scratch_shapes=[
            pltpu.VMEM((devices * rows, width), jnp.bfloat16),
            pltpu.VMEM((out_panel, in_panel), jnp.float32),
        ],
        compiler_params=pltpu.CompilerParams(vmem_limit_bytes=16 * 2**20),
    )(me, *pieces)
    return corrected, score.reshape(balanced)


def ringed(activations, out_grads, slot_of_row, basis_in, basis_out):
    devices = lax.axis_size("dp")
    chips = devices // 2
    own_index = lax.axis_index("dp")
    rows = activations.shape[0]
    balanced = rows // 2
    depth_in, width = basis_in.shape
    depth_out = basis_out.shape[0]

    order = ring_order(chips)

    def ring(step):
        pairs = []
        for i, chip in enumerate(order):
            to = order[(i + step) % chips]
            pairs += [(2 * chip, 2 * to), (2 * chip + 1, 2 * to + 1)]
        return pairs

    forward, backward = ring(1), ring(-1)
    swap = [(i, i ^ 1) for i in range(devices)]

    def send(x, pairs):
        return lax.ppermute(x, "dp", pairs)

    half = chips // 2
    distances = [0]
    for d in range(1, half):
        distances += [d, -d]
    distances += [half]

    chip = own_index // 2
    position = jnp.where(chip % 2 == 0, chip // 2, chips - 1 - chip // 2)
    from_position = (position - jnp.array(distances, jnp.int32)) % chips
    owners = jnp.where(
        from_position < half, 2 * from_position, 2 * (chips - 1 - from_position) + 1
    ) * 2 + own_index % 2

    cut = (depth_in + depth_out) // 2
    second = basis_out[cut - depth_in :]
    first = lax.pad(basis_out, basis_out.dtype.type(0), ((depth_in, -second.shape[0], 0), (0, 0, 0)))
    first = lax.dynamic_update_slice(first, basis_in, (0, 0))
    first, second = {0: first}, {0: second}

    def hop(ahead, behind, s):
        ahead[s] = send(ahead[s - 1], forward)
        behind[-s] = send(behind[1 - s], backward)

    def pieces(held, at):
        return [(distances.index(d), 0 if held is first else cut, held[d]) for d in at]

    def add(kinds, parts, totals):
        tokens = [(activations, swapped_act), (out_grads, swapped_grad)]
        return list(project(owners, kinds, tokens, parts, totals, (depth_in, depth_out)))

    def after(held, at, totals):
        got = lax.optimization_barrier(tuple(held[d] for d in at) + tuple(totals))
        for d, x in zip(at, got):
            held[d] = x
        return list(got[len(at) :])

    swapped_act, swapped_grad = send(activations, swap), send(out_grads, swap)
    hop(first, second, 1)
    second[1] = send(second[0], forward)
    ready, swapped_act = lax.optimization_barrier((first[0], swapped_act))
    first[-1] = send(ready, backward)
    zero = jnp.zeros((rows, width), jnp.float32)
    grad = [zero, zero]
    for s in range(1, half):
        own = pieces(first, [0]) + pieces(second, [0]) if s == 1 else []
        if s + 1 < half:
            hop(first, second, s + 1)
        else:
            first[half], second[half] = send(first[s], forward), send(second[-s], backward)
        grad = add((1,), own + pieces(first, [s]) + pieces(second, [-s]), grad)
        grad = after(second, [s], after(first, [-s], grad))
        if s + 1 < half:
            hop(second, first, s + 1)
        grad = add((1,), pieces(second, [s]) + pieces(first, [-s]), grad)
        if s + 1 < half:
            grad = after(first, [s + 1], after(second, [-s - 1], grad))
    act = add((0,), pieces(first, distances[:-1]), [zero, zero])
    tokens = (activations, out_grads, swapped_act, swapped_grad)
    block, *act = fetch(owners, chips - 1, tokens, depth_in, depth_out, act)
    panels = (first[half], second[half])
    theirs = finish_dots(block[1], panels, act[1], grad[1], depth_in)
    block[0], swapped = lax.optimization_barrier((block[0], theirs))
    swapped = send(swapped, swap)
    mine = finish_dots(block[0], panels, act[0], grad[0], depth_in)

    is_valid = slot_of_row >= 0
    owner = jnp.where(is_valid, slot_of_row // balanced, -1)
    tag = jnp.concatenate([owner, slot_of_row % balanced]).astype(jnp.bfloat16)
    tag = jnp.broadcast_to(jnp.pad(tag, (0, 2 * width - 2 * rows))[None, :], (16, 2 * width))
    rotated = mine + swapped
    counts = is_valid[:, None] | (jnp.arange(2 * width) < width)[None, :]
    squares = jnp.where(counts, rotated * rotated, 0.0).astype(jnp.bfloat16)

    held = {0: jnp.concatenate([squares, tag], axis=0)}
    for s in range(1, half):
        hop(held, held, s)
    middle = (rows + 16) // 32 * 16
    upper = send(held[half - 2][:middle], ring(2))
    lower = send(held[2 - half][middle:], ring(-2))
    held[half - 1], held[1 - half], upper, lower = lax.optimization_barrier(
        (held[half - 1], held[1 - half], upper, lower)
    )
    near = jnp.concatenate([held[d] for d in distances[:-3]], axis=0)
    far = jnp.concatenate([held[half - 1], held[1 - half], upper, lower], axis=0)
    own = [near, far]
    swapped = [send(x, swap) for x in own]
    return last(own_index[None], own + swapped, rows, width, devices, balanced)


def body(*arrays):
    if lax.axis_size("dp") == 16:
        return ringed(*arrays)
    return gathered(*arrays)


def solution(mesh):
    return jax.shard_map(
        body,
        mesh=mesh,
        in_specs=(
            P(("groups", "dp"), None),
            P(("groups", "dp"), None),
            P(("groups", "dp")),
            P(("groups", "dp"), None),
            P(("groups", "dp"), None),
        ),
        out_specs=(P(("groups", "dp"), None), P(("groups", "dp"))),
        check_vma=False,
    )
```

```python
import functools

import jax
import jax.numpy as jnp
from jax import lax
from jax.experimental import pallas as pl
from jax.experimental.pallas import tpu as pltpu
from jax.sharding import PartitionSpec as P

damping = 0.1


def ring_order(chips):
    if chips == 8:
        return [0, 2, 4, 6, 7, 5, 3, 1]
    return list(range(chips))


def dot(a, b):
    return jnp.dot(a, b, preferred_element_type=jnp.float32)


def squared(x):
    return (x * x).astype(jnp.bfloat16)


def finish(all_grad, all_act, owners, places, own_index, devices, balanced):
    out_panel, in_panel = all_grad.shape[1], all_act.shape[1]
    masked = jnp.where(owners[:, None] >= 0, all_grad, jnp.zeros_like(all_grad))
    corrected = lax.dot_general(
        masked, all_act, (((0,), (0,)), ((), ())), preferred_element_type=jnp.float32
    ) / (devices * balanced)
    inverse = 1.0 / (corrected + damping)
    wanted = jnp.arange(balanced, dtype=jnp.int32)
    pick = ((owners[None, :] == own_index) & (places[None, :] == wanted[:, None])).astype(jnp.bfloat16)
    own_grad = dot(pick, all_grad)
    own_act = dot(pick, all_act)
    weighted = lax.dot_general(
        own_act, inverse, (((1,), (1,)), ((), ())), precision=lax.Precision.HIGHEST
    )
    self_score = jnp.sum(own_grad * weighted, axis=1) / (out_panel * in_panel)
    panel_rows = out_panel // devices
    own_corrected = lax.dynamic_slice(corrected, (own_index * panel_rows, 0), (panel_rows, in_panel))
    return own_corrected, self_score


def gathered(activations, out_grads, slot_of_row, basis_in, basis_out):
    devices = lax.axis_size("dp")
    own_index = lax.axis_index("dp")
    balanced = activations.shape[0] // 2

    def everyone(x):
        return lax.all_gather(x, "dp", axis=0, tiled=True)

    act_sq = squared(dot(activations, everyone(basis_in)))
    grad_sq = squared(dot(out_grads, everyone(basis_out)))
    slots = everyone(slot_of_row)
    owners = jnp.where(slots >= 0, slots // balanced, -1)
    return finish(
        everyone(grad_sq), everyone(act_sq), owners, slots % balanced, own_index, devices, balanced
    )


def runs(first, count, depth_in, depth_out):
    inside = max(0, min(depth_in - first, count))
    found = []
    if inside:
        found.append((0, first, inside, 0))
    if count > inside:
        found.append((1, first + inside - depth_in, count - inside, inside))
    return found


def project_kernel(kinds, parts, depths, owners_ref, *refs):
    sources, refs = refs[: 2 * len(kinds)], refs[2 * len(kinds) :]
    panels, refs = refs[: len(parts)], refs[len(parts) :]
    before, (mine_out, theirs_out, block, sems) = refs[: 2 * len(kinds)], refs[2 * len(kinds) :]
    rows, width = sources[0].shape[0], panels[0].shape[1]
    work, at = [], 0
    for (slot, first), panel in zip(parts, panels):
        for kind, start, count, within in runs(first, panel.shape[0], *depths):
            if kind not in kinds:
                continue
            column = pl.multiple_of(owners_ref[slot] * depths[kind] + start, 128)
            copies = []
            for j in range(2):
                copy = pltpu.make_async_copy(
                    sources[2 * kinds.index(kind) + j].at[:, pl.ds(column, count)],
                    block.at[pl.ds(j * rows, rows), pl.ds(at, count)],
                    sems.at[len(work), j],
                )
                copy.start()
                copies.append(copy)
            work.append((kind, at, count, panel.at[pl.ds(within, count), :], copies))
            at += count
    totals = {}
    for kind, at, count, panel, copies in work:
        for copy in copies:
            copy.wait()
        totals[kind] = totals.get(kind, 0.0) + dot(block[:, at : at + count], panel[...])
    for i, kind in enumerate(kinds):
        columns = slice(i * width, (i + 1) * width)
        mine_out[:, columns] = before[2 * i][...] + totals[kind][:rows]
        theirs_out[:, columns] = before[2 * i + 1][...] + totals[kind][rows:]


def project(owners, kinds, tokens, parts, before, depths):
    sources = [x for kind in kinds for x in tokens[kind]]
    rows, width = sources[0].shape[0], parts[0][2].shape[1]
    panels = [p[2] for p in parts]
    counts = [
        run[2] for p in parts for run in runs(p[1], p[2].shape[0], *depths) if run[0] in kinds
    ]
    vmem = pl.BlockSpec(memory_space=pltpu.VMEM)
    total = jax.ShapeDtypeStruct((rows, len(kinds) * width), jnp.float32)
    return pl.pallas_call(
        functools.partial(project_kernel, kinds, [p[:2] for p in parts], depths),
        out_shape=(total, total),
        in_specs=[pl.BlockSpec(memory_space=pltpu.SMEM)]
        + [pl.BlockSpec(memory_space=pl.ANY)] * len(sources)
        + [vmem] * (len(parts) + len(before)),
        out_specs=(vmem, vmem),
        scratch_shapes=[
            pltpu.VMEM((2 * rows, sum(counts)), sources[0].dtype),
            pltpu.SemaphoreType.DMA((len(counts), 2)),
        ],
        compiler_params=pltpu.CompilerParams(vmem_limit_bytes=16 * 2**20),
        cost_estimate=pl.CostEstimate(flops=1, bytes_accessed=1, transcendentals=0),
    )(
        owners,
        *[pltpu.with_memory_space_constraint(x, pltpu.HBM) for x in sources],
        *[pltpu.with_memory_space_constraint(x, pltpu.VMEM) for x in panels],
        *before,
    )


def copy_all(copies):
    for copy in copies:
        copy.start()
    for copy in copies:
        copy.wait()


def halves_kernel(upper_ref, lower_ref, first_ref, second_ref, sems):
    above, rest = upper_ref.shape[0], first_ref.shape[0] - upper_ref.shape[0]
    copy_all([
        pltpu.make_async_copy(
            lower_ref.at[pl.ds(rest, second_ref.shape[0]), :], second_ref, sems.at[0]
        ),
        pltpu.make_async_copy(upper_ref, first_ref.at[pl.ds(0, above), :], sems.at[1]),
        pltpu.make_async_copy(
            lower_ref.at[pl.ds(0, rest), :], first_ref.at[pl.ds(above, rest), :], sems.at[2]
        ),
    ])


def halves(upper, lower, cut):
    total, width = upper.shape[0] + lower.shape[0], upper.shape[1]
    vmem = pl.BlockSpec(memory_space=pltpu.VMEM)
    return pl.pallas_call(
        halves_kernel,
        out_shape=(
            jax.ShapeDtypeStruct((cut, width), upper.dtype),
            jax.ShapeDtypeStruct((total - cut, width), upper.dtype),
        ),
        in_specs=[pl.BlockSpec(memory_space=pl.ANY)] * 2,
        out_specs=(vmem, vmem),
        scratch_shapes=[pltpu.SemaphoreType.DMA((3,))],
        compiler_params=pltpu.CompilerParams(vmem_limit_bytes=16 * 2**20),
    )(*[pltpu.with_memory_space_constraint(x, pltpu.HBM) for x in (upper, lower)])


def fetch_kernel(slot, depths, owners_ref, *refs):
    sources, (own_ref, sibling_ref, sems) = refs[:4], refs[4:7]
    copies, at = [], 0
    for kind, depth in enumerate(depths):
        column = pl.multiple_of(owners_ref[slot] * depth, 128)
        for j, block in enumerate((own_ref, sibling_ref)):
            copies.append(
                pltpu.make_async_copy(
                    sources[2 * j + kind].at[:, pl.ds(column, depth)],
                    block.at[:, pl.ds(at, depth)],
                    sems.at[kind, j],
                )
            )
        at += depth
    copy_all(copies)


def fetch(owners, slot, tokens, depth_in, depth_out, after):
    rows = tokens[0].shape[0]
    vmem = pl.BlockSpec(memory_space=pltpu.VMEM)
    block = jax.ShapeDtypeStruct((rows, depth_in + depth_out), tokens[0].dtype)
    got = pl.pallas_call(
        functools.partial(fetch_kernel, slot, (depth_in, depth_out)),
        out_shape=(block, block),
        in_specs=[pl.BlockSpec(memory_space=pltpu.SMEM)] + [pl.BlockSpec(memory_space=pl.ANY)] * 4,
        out_specs=(vmem, vmem),
        scratch_shapes=[pltpu.SemaphoreType.DMA((2, 2))],
        compiler_params=pltpu.CompilerParams(vmem_limit_bytes=16 * 2**20),
        cost_estimate=pl.CostEstimate(flops=1, bytes_accessed=1, transcendentals=0),
    )(owners, *[pltpu.with_memory_space_constraint(x, pltpu.HBM) for x in tokens])
    return [list(got), *after]


def finish_dots_kernel(depth_in, block_ref, first_ref, second_ref, act_ref, grad_ref, out_ref):
    cut, width = first_ref.shape
    out_ref[:, :width] = act_ref[...] + dot(block_ref[:, :depth_in], first_ref[:depth_in, :])
    out_ref[:, width:] = (
        grad_ref[...]
        + dot(block_ref[:, depth_in:cut], first_ref[depth_in:, :])
        + dot(block_ref[:, cut:], second_ref[...])
    )


def finish_dots(block, panels, act, grad, depth_in):
    rows, width = act.shape
    vmem = pl.BlockSpec(memory_space=pltpu.VMEM)
    return pl.pallas_call(
        functools.partial(finish_dots_kernel, depth_in),
        out_shape=jax.ShapeDtypeStruct((rows, 2 * width), jnp.float32),
        in_specs=[vmem] * 5,
        out_specs=vmem,
        compiler_params=pltpu.CompilerParams(vmem_limit_bytes=16 * 2**20),
        cost_estimate=pl.CostEstimate(flops=1, bytes_accessed=1, transcendentals=0),
    )(block, *[pltpu.with_memory_space_constraint(x, pltpu.VMEM) for x in panels], act, grad)


def add_up(me, pieces, squares, rows, width, balanced):
    wanted = lax.broadcasted_iota(jnp.int32, (balanced, rows), 0)
    at, picks = 0, []
    for piece in pieces:
        for start in range(0, piece.shape[0], rows + 16):
            squares[at : at + rows, :] = piece[start : start + rows, :]
            tag = piece[start + rows : start + rows + 16, :][:1].astype(jnp.float32).astype(jnp.int32)
            owner, place = tag[:, :rows], tag[:, rows : 2 * rows]
            picks.append(((owner == me) & (place == wanted)).astype(jnp.float32))
            at += rows
    pick = jnp.concatenate(picks, axis=1).astype(jnp.bfloat16)
    act, grad = squares[:, :width], squares[:, width:]
    return (
        lax.dot_general(grad, act, (((0,), (0,)), ((), ())), preferred_element_type=jnp.float32),
        dot(pick, act),
        lax.dot_general(grad, pick, (((0,), (1,)), ((), ())), preferred_element_type=jnp.float32),
    )


def some_sums_kernel(rows, me_ref, *refs):
    pieces, (total_ref, act_ref, grad_ref, squares) = refs[:-4], refs[-4:]
    balanced, width = act_ref.shape
    total_ref[...], act_ref[...], grad_ref[...] = add_up(
        me_ref[0], pieces, squares, rows, width, balanced
    )


def some_sums(me, pieces, rows, width, balanced):
    vmem = pl.BlockSpec(memory_space=pltpu.VMEM)
    tokens = sum(piece.shape[0] for piece in pieces) // (rows + 16) * rows
    out_panel = pieces[0].shape[1] - width
    return pl.pallas_call(
        functools.partial(some_sums_kernel, rows),
        out_shape=(
            jax.ShapeDtypeStruct((out_panel, width), jnp.float32),
            jax.ShapeDtypeStruct((balanced, width), jnp.float32),
            jax.ShapeDtypeStruct((out_panel, balanced), jnp.float32),
        ),
        in_specs=[pl.BlockSpec(memory_space=pltpu.SMEM)] + [vmem] * len(pieces),
        out_specs=(vmem, vmem, vmem),
        scratch_shapes=[pltpu.VMEM((tokens, pieces[0].shape[1]), jnp.bfloat16)],
        compiler_params=pltpu.CompilerParams(vmem_limit_bytes=16 * 2**20),
        cost_estimate=pl.CostEstimate(flops=1, bytes_accessed=1, transcendentals=0),
    )(me, *pieces)


def last_kernel(rows, scale, me_ref, first_ref, second_ref, total_ref, act_ref, grad_ref, *refs):
    corrected_ref, score_ref, squares, held = refs
    me = me_ref[0]
    panel_rows, in_panel = corrected_ref.shape
    out_panel = total_ref.shape[0]
    total, own_act, own_grad = add_up(
        me, (first_ref, second_ref), squares, rows, in_panel, act_ref.shape[0]
    )
    corrected = (total + total_ref[...]) * scale
    held[...] = corrected
    corrected_ref[...] = held[pl.ds(pl.multiple_of(me * panel_rows, panel_rows), panel_rows), :]
    inverse = 1.0 / (corrected + damping)
    high = inverse.astype(jnp.bfloat16)
    low = (inverse - high.astype(jnp.float32)).astype(jnp.bfloat16)
    own_act = (own_act + act_ref[...]).astype(jnp.bfloat16)
    weighted = sum(
        lax.dot_general(part, own_act, (((1,), (1,)), ((), ())), preferred_element_type=jnp.float32)
        for part in (high, low)
    )
    score = jnp.sum((own_grad + grad_ref[...]) * weighted, axis=0, keepdims=True)
    score_ref[...] = score / (out_panel * in_panel)


def last(me, pieces, sums, rows, devices):
    vmem = pl.BlockSpec(memory_space=pltpu.VMEM)
    (out_panel, in_panel), balanced = sums[0].shape, sums[1].shape[0]
    tokens = sum(piece.shape[0] for piece in pieces) // (rows + 16) * rows
    corrected, score = pl.pallas_call(
        functools.partial(last_kernel, rows, 1.0 / (devices * balanced)),
        out_shape=(
            jax.ShapeDtypeStruct((out_panel // devices, in_panel), jnp.float32),
            jax.ShapeDtypeStruct((1, balanced), jnp.float32),
        ),
        in_specs=[pl.BlockSpec(memory_space=pltpu.SMEM)] + [vmem] * 5,
        out_specs=(vmem, vmem),
        scratch_shapes=[
            pltpu.VMEM((tokens, out_panel + in_panel), jnp.bfloat16),
            pltpu.VMEM((out_panel, in_panel), jnp.float32),
        ],
        compiler_params=pltpu.CompilerParams(vmem_limit_bytes=16 * 2**20),
    )(me, *pieces, *sums)
    return corrected, score.reshape(balanced)


def ringed(activations, out_grads, slot_of_row, basis_in, basis_out):
    devices = lax.axis_size("dp")
    chips = devices // 2
    own_index = lax.axis_index("dp")
    rows = activations.shape[0]
    balanced = rows // 2
    depth_in, width = basis_in.shape
    depth_out = basis_out.shape[0]

    order = ring_order(chips)

    def ring(step):
        pairs = []
        for i, chip in enumerate(order):
            to = order[(i + step) % chips]
            pairs += [(2 * chip, 2 * to), (2 * chip + 1, 2 * to + 1)]
        return pairs

    forward, backward = ring(1), ring(-1)
    swap = [(i, i ^ 1) for i in range(devices)]

    def send(x, pairs):
        return lax.ppermute(x, "dp", pairs)

    half = chips // 2
    distances = [0]
    for d in range(1, half):
        distances += [d, -d]
    distances += [half]

    chip = own_index // 2
    position = jnp.where(chip % 2 == 0, chip // 2, chips - 1 - chip // 2)
    from_position = (position - jnp.array(distances, jnp.int32)) % chips
    owners = jnp.where(
        from_position < half, 2 * from_position, 2 * (chips - 1 - from_position) + 1
    ) * 2 + own_index % 2

    cut = (depth_in + depth_out) // 2
    second = basis_out[cut - depth_in :]
    first = lax.pad(basis_out, basis_out.dtype.type(0), ((depth_in, -second.shape[0], 0), (0, 0, 0)))
    first = lax.dynamic_update_slice(first, basis_in, (0, 0))
    first, second = {0: first}, {0: second}

    def hop(ahead, behind, s):
        ahead[s] = send(ahead[s - 1], forward)
        behind[-s] = send(behind[1 - s], backward)

    def pieces(held, at):
        return [(distances.index(d), 0 if held is first else cut, held[d]) for d in at]

    def add(kinds, parts, totals):
        tokens = [(activations, swapped_act), (out_grads, swapped_grad)]
        return list(project(owners, kinds, tokens, parts, totals, (depth_in, depth_out)))

    def after(held, at, totals):
        got = lax.optimization_barrier(tuple(held[d] for d in at) + tuple(totals))
        for d, x in zip(at, got):
            held[d] = x
        return list(got[len(at) :])

    swapped_act, swapped_grad = send(activations, swap), send(out_grads, swap)
    hop(first, second, 1)
    second[1] = send(second[0], forward)
    ready, swapped_act = lax.optimization_barrier((first[0], swapped_act))
    first[-1] = send(ready, backward)
    zero = jnp.zeros((rows, width), jnp.float32)
    grad = [zero, zero]
    for s in range(1, half):
        own = pieces(first, [0]) + pieces(second, [0]) if s == 1 else []
        if s + 1 < half:
            hop(first, second, s + 1)
        else:
            first[half], second[half] = send(first[s], forward), send(second[-s], backward)
        grad = add((1,), own + pieces(first, [s]) + pieces(second, [-s]), grad)
        grad = after(second, [s], after(first, [-s], grad))
        if s + 1 < half:
            hop(second, first, s + 1)
        grad = add((1,), pieces(second, [s]) + pieces(first, [-s]), grad)
        if s + 1 < half:
            grad = after(first, [s + 1], after(second, [-s - 1], grad))
    act = add((0,), pieces(first, distances[:-1]), [zero, zero])
    tokens = (activations, out_grads, swapped_act, swapped_grad)
    block, *act = fetch(owners, chips - 1, tokens, depth_in, depth_out, act)
    panels = (first[half], second[half])
    theirs = finish_dots(block[1], panels, act[1], grad[1], depth_in)
    block[0], swapped = lax.optimization_barrier((block[0], theirs))
    swapped = send(swapped, swap)
    mine = finish_dots(block[0], panels, act[0], grad[0], depth_in)

    is_valid = slot_of_row >= 0
    owner = jnp.where(is_valid, slot_of_row // balanced, -1)
    tag = jnp.concatenate([owner, slot_of_row % balanced]).astype(jnp.bfloat16)
    tag = jnp.broadcast_to(jnp.pad(tag, (0, 2 * width - 2 * rows))[None, :], (16, 2 * width))
    rotated = mine + swapped
    counts = is_valid[:, None] | (jnp.arange(2 * width) < width)[None, :]
    squares = jnp.where(counts, rotated * rotated, 0.0).astype(jnp.bfloat16)

    held = {0: jnp.concatenate([squares, tag], axis=0)}
    for s in range(1, half):
        hop(held, held, s)
    middle = (rows + 16) // 32 * 16
    upper = send(held[half - 2][:middle], ring(2))
    lower = send(held[2 - half][middle:], ring(-2))
    held[half - 1], held[1 - half], upper, lower = lax.optimization_barrier(
        (held[half - 1], held[1 - half], upper, lower)
    )
    near = jnp.concatenate([held[-d] for d in distances[:-3]], axis=0)
    far = jnp.concatenate([held[half - 1], held[1 - half], upper, lower], axis=0)
    own = [near, far]
    swapped = [send(x, swap) for x in own]
    me = own_index[None]
    near_both = lax.optimization_barrier((near, swapped[0], far))[:2]
    sums = some_sums(me, list(near_both), rows, width, balanced)
    return last(me, [far, swapped[1]], sums, rows, devices)


def body(*arrays):
    if lax.axis_size("dp") == 16:
        return ringed(*arrays)
    return gathered(*arrays)


def solution(mesh):
    return jax.shard_map(
        body,
        mesh=mesh,
        in_specs=(
            P(("groups", "dp"), None),
            P(("groups", "dp"), None),
            P(("groups", "dp")),
            P(("groups", "dp"), None),
            P(("groups", "dp"), None),
        ),
        out_specs=(P(("groups", "dp"), None), P(("groups", "dp"))),
        check_vma=False,
    )
```

```python
import functools

import jax
import jax.numpy as jnp
from jax import lax
from jax.experimental import pallas as pl
from jax.experimental.pallas import tpu as pltpu
from jax.sharding import PartitionSpec as P

damping = 0.1


def ring_order(chips):
    if chips == 8:
        return [0, 2, 4, 6, 7, 5, 3, 1]
    return list(range(chips))


def dot(a, b):
    return jnp.dot(a, b, preferred_element_type=jnp.float32)


def squared(x):
    return (x * x).astype(jnp.bfloat16)


def finish(all_grad, all_act, owners, places, own_index, devices, balanced):
    out_panel, in_panel = all_grad.shape[1], all_act.shape[1]
    masked = jnp.where(owners[:, None] >= 0, all_grad, jnp.zeros_like(all_grad))
    corrected = lax.dot_general(
        masked, all_act, (((0,), (0,)), ((), ())), preferred_element_type=jnp.float32
    ) / (devices * balanced)
    inverse = 1.0 / (corrected + damping)
    wanted = jnp.arange(balanced, dtype=jnp.int32)
    pick = ((owners[None, :] == own_index) & (places[None, :] == wanted[:, None])).astype(jnp.bfloat16)
    own_grad = dot(pick, all_grad)
    own_act = dot(pick, all_act)
    weighted = lax.dot_general(
        own_act, inverse, (((1,), (1,)), ((), ())), precision=lax.Precision.HIGHEST
    )
    self_score = jnp.sum(own_grad * weighted, axis=1) / (out_panel * in_panel)
    panel_rows = out_panel // devices
    own_corrected = lax.dynamic_slice(corrected, (own_index * panel_rows, 0), (panel_rows, in_panel))
    return own_corrected, self_score


def gathered(activations, out_grads, slot_of_row, basis_in, basis_out):
    devices = lax.axis_size("dp")
    own_index = lax.axis_index("dp")
    balanced = activations.shape[0] // 2

    def everyone(x):
        return lax.all_gather(x, "dp", axis=0, tiled=True)

    act_sq = squared(dot(activations, everyone(basis_in)))
    grad_sq = squared(dot(out_grads, everyone(basis_out)))
    slots = everyone(slot_of_row)
    owners = jnp.where(slots >= 0, slots // balanced, -1)
    return finish(
        everyone(grad_sq), everyone(act_sq), owners, slots % balanced, own_index, devices, balanced
    )


def runs(first, count, depth_in, depth_out):
    inside = max(0, min(depth_in - first, count))
    found = []
    if inside:
        found.append((0, first, inside, 0))
    if count > inside:
        found.append((1, first + inside - depth_in, count - inside, inside))
    return found


def project_kernel(kinds, parts, depths, owners_ref, *refs):
    sources, refs = refs[: 2 * len(kinds)], refs[2 * len(kinds) :]
    panels, refs = refs[: len(parts)], refs[len(parts) :]
    before, (mine_out, theirs_out, block, sems) = refs[: 2 * len(kinds)], refs[2 * len(kinds) :]
    rows, width = sources[0].shape[0], panels[0].shape[1]
    work, at = [], 0
    for (slot, first), panel in zip(parts, panels):
        for kind, start, count, within in runs(first, panel.shape[0], *depths):
            if kind not in kinds:
                continue
            column = pl.multiple_of(owners_ref[slot] * depths[kind] + start, 128)
            copies = []
            for j in range(2):
                copy = pltpu.make_async_copy(
                    sources[2 * kinds.index(kind) + j].at[:, pl.ds(column, count)],
                    block.at[pl.ds(j * rows, rows), pl.ds(at, count)],
                    sems.at[len(work), j],
                )
                copy.start()
                copies.append(copy)
            work.append((kind, at, count, panel.at[pl.ds(within, count), :], copies))
            at += count
    totals = {}
    for kind, at, count, panel, copies in work:
        for copy in copies:
            copy.wait()
        totals[kind] = totals.get(kind, 0.0) + dot(block[:, at : at + count], panel[...])
    for i, kind in enumerate(kinds):
        columns = slice(i * width, (i + 1) * width)
        mine_out[:, columns] = before[2 * i][...] + totals[kind][:rows]
        theirs_out[:, columns] = before[2 * i + 1][...] + totals[kind][rows:]


def project(owners, kinds, tokens, parts, before, depths):
    sources = [x for kind in kinds for x in tokens[kind]]
    rows, width = sources[0].shape[0], parts[0][2].shape[1]
    panels = [p[2] for p in parts]
    counts = [
        run[2] for p in parts for run in runs(p[1], p[2].shape[0], *depths) if run[0] in kinds
    ]
    vmem = pl.BlockSpec(memory_space=pltpu.VMEM)
    total = jax.ShapeDtypeStruct((rows, len(kinds) * width), jnp.float32)
    return pl.pallas_call(
        functools.partial(project_kernel, kinds, [p[:2] for p in parts], depths),
        out_shape=(total, total),
        in_specs=[pl.BlockSpec(memory_space=pltpu.SMEM)]
        + [pl.BlockSpec(memory_space=pl.ANY)] * len(sources)
        + [vmem] * (len(parts) + len(before)),
        out_specs=(vmem, vmem),
        scratch_shapes=[
            pltpu.VMEM((2 * rows, sum(counts)), sources[0].dtype),
            pltpu.SemaphoreType.DMA((len(counts), 2)),
        ],
        compiler_params=pltpu.CompilerParams(vmem_limit_bytes=16 * 2**20),
        cost_estimate=pl.CostEstimate(flops=1, bytes_accessed=1, transcendentals=0),
    )(
        owners,
        *[pltpu.with_memory_space_constraint(x, pltpu.HBM) for x in sources],
        *[pltpu.with_memory_space_constraint(x, pltpu.VMEM) for x in panels],
        *before,
    )


def copy_all(copies):
    for copy in copies:
        copy.start()
    for copy in copies:
        copy.wait()


def halves_kernel(upper_ref, lower_ref, first_ref, second_ref, sems):
    above, rest = upper_ref.shape[0], first_ref.shape[0] - upper_ref.shape[0]
    copy_all([
        pltpu.make_async_copy(
            lower_ref.at[pl.ds(rest, second_ref.shape[0]), :], second_ref, sems.at[0]
        ),
        pltpu.make_async_copy(upper_ref, first_ref.at[pl.ds(0, above), :], sems.at[1]),
        pltpu.make_async_copy(
            lower_ref.at[pl.ds(0, rest), :], first_ref.at[pl.ds(above, rest), :], sems.at[2]
        ),
    ])


def halves(upper, lower, cut):
    total, width = upper.shape[0] + lower.shape[0], upper.shape[1]
    vmem = pl.BlockSpec(memory_space=pltpu.VMEM)
    return pl.pallas_call(
        halves_kernel,
        out_shape=(
            jax.ShapeDtypeStruct((cut, width), upper.dtype),
            jax.ShapeDtypeStruct((total - cut, width), upper.dtype),
        ),
        in_specs=[pl.BlockSpec(memory_space=pl.ANY)] * 2,
        out_specs=(vmem, vmem),
        scratch_shapes=[pltpu.SemaphoreType.DMA((3,))],
        compiler_params=pltpu.CompilerParams(vmem_limit_bytes=16 * 2**20),
    )(*[pltpu.with_memory_space_constraint(x, pltpu.HBM) for x in (upper, lower)])


def fetch_kernel(slot, depths, owners_ref, *refs):
    sources, (own_ref, sibling_ref, sems) = refs[:4], refs[4:7]
    copies, at = [], 0
    for kind, depth in enumerate(depths):
        column = pl.multiple_of(owners_ref[slot] * depth, 128)
        for j, block in enumerate((own_ref, sibling_ref)):
            copies.append(
                pltpu.make_async_copy(
                    sources[2 * j + kind].at[:, pl.ds(column, depth)],
                    block.at[:, pl.ds(at, depth)],
                    sems.at[kind, j],
                )
            )
        at += depth
    copy_all(copies)


def fetch(owners, slot, tokens, depth_in, depth_out, after):
    rows = tokens[0].shape[0]
    vmem = pl.BlockSpec(memory_space=pltpu.VMEM)
    block = jax.ShapeDtypeStruct((rows, depth_in + depth_out), tokens[0].dtype)
    got = pl.pallas_call(
        functools.partial(fetch_kernel, slot, (depth_in, depth_out)),
        out_shape=(block, block),
        in_specs=[pl.BlockSpec(memory_space=pltpu.SMEM)] + [pl.BlockSpec(memory_space=pl.ANY)] * 4,
        out_specs=(vmem, vmem),
        scratch_shapes=[pltpu.SemaphoreType.DMA((2, 2))],
        compiler_params=pltpu.CompilerParams(vmem_limit_bytes=16 * 2**20),
        cost_estimate=pl.CostEstimate(flops=1, bytes_accessed=1, transcendentals=0),
    )(owners, *[pltpu.with_memory_space_constraint(x, pltpu.HBM) for x in tokens])
    return [list(got), *after]


def finish_dots_kernel(depth_in, block_ref, first_ref, second_ref, act_ref, grad_ref, out_ref):
    cut, width = first_ref.shape
    out_ref[:, :width] = act_ref[...] + dot(block_ref[:, :depth_in], first_ref[:depth_in, :])
    out_ref[:, width:] = (
        grad_ref[...]
        + dot(block_ref[:, depth_in:cut], first_ref[depth_in:, :])
        + dot(block_ref[:, cut:], second_ref[...])
    )


def finish_dots(block, panels, act, grad, depth_in):
    rows, width = act.shape
    vmem = pl.BlockSpec(memory_space=pltpu.VMEM)
    return pl.pallas_call(
        functools.partial(finish_dots_kernel, depth_in),
        out_shape=jax.ShapeDtypeStruct((rows, 2 * width), jnp.float32),
        in_specs=[vmem] * 5,
        out_specs=vmem,
        compiler_params=pltpu.CompilerParams(vmem_limit_bytes=16 * 2**20),
        cost_estimate=pl.CostEstimate(flops=1, bytes_accessed=1, transcendentals=0),
    )(block, *[pltpu.with_memory_space_constraint(x, pltpu.VMEM) for x in panels], act, grad)


def add_up(me, pieces, squares, rows, width, balanced):
    wanted = lax.broadcasted_iota(jnp.int32, (balanced, rows), 0)
    at, picks = 0, []
    for piece in pieces:
        for start in range(0, piece.shape[0], rows + 16):
            squares[at : at + rows, :] = piece[start : start + rows, :]
            tag = piece[start + rows : start + rows + 16, :][:1].astype(jnp.float32).astype(jnp.int32)
            owner, place = tag[:, :rows], tag[:, rows : 2 * rows]
            picks.append(((owner == me) & (place == wanted)).astype(jnp.float32))
            at += rows
    pick = jnp.concatenate(picks, axis=1).astype(jnp.bfloat16)
    act, grad = squares[:, :width], squares[:, width:]
    return (
        lax.dot_general(grad, act, (((0,), (0,)), ((), ())), preferred_element_type=jnp.float32),
        dot(pick, act),
        lax.dot_general(grad, pick, (((0,), (1,)), ((), ())), preferred_element_type=jnp.float32),
    )


def some_sums_kernel(rows, me_ref, *refs):
    pieces, (total_ref, act_ref, grad_ref, squares) = refs[:-4], refs[-4:]
    balanced, width = act_ref.shape
    total_ref[...], act_ref[...], grad_ref[...] = add_up(
        me_ref[0], pieces, squares, rows, width, balanced
    )


def some_sums(me, pieces, rows, width, balanced):
    vmem = pl.BlockSpec(memory_space=pltpu.VMEM)
    tokens = sum(piece.shape[0] for piece in pieces) // (rows + 16) * rows
    out_panel = pieces[0].shape[1] - width
    return pl.pallas_call(
        functools.partial(some_sums_kernel, rows),
        out_shape=(
            jax.ShapeDtypeStruct((out_panel, width), jnp.float32),
            jax.ShapeDtypeStruct((balanced, width), jnp.float32),
            jax.ShapeDtypeStruct((out_panel, balanced), jnp.float32),
        ),
        in_specs=[pl.BlockSpec(memory_space=pltpu.SMEM)] + [vmem] * len(pieces),
        out_specs=(vmem, vmem, vmem),
        scratch_shapes=[pltpu.VMEM((tokens, pieces[0].shape[1]), jnp.bfloat16)],
        compiler_params=pltpu.CompilerParams(vmem_limit_bytes=16 * 2**20),
        cost_estimate=pl.CostEstimate(flops=1, bytes_accessed=1, transcendentals=0),
    )(me, *pieces)


def last_kernel(rows, scale, me_ref, piece_ref, total_ref, act_ref, grad_ref, *refs):
    corrected_ref, score_ref, squares, held = refs
    me = me_ref[0]
    panel_rows, in_panel = corrected_ref.shape
    out_panel = total_ref.shape[0]
    total, own_act, own_grad = add_up(
        me, (piece_ref,), squares, rows, in_panel, act_ref.shape[0]
    )
    corrected = (total + total_ref[...]) * scale
    held[...] = corrected
    corrected_ref[...] = held[pl.ds(pl.multiple_of(me * panel_rows, panel_rows), panel_rows), :]
    inverse = 1.0 / (corrected + damping)
    high = inverse.astype(jnp.bfloat16)
    low = (inverse - high.astype(jnp.float32)).astype(jnp.bfloat16)
    own_act = (own_act + act_ref[...]).astype(jnp.bfloat16)
    weighted = sum(
        lax.dot_general(part, own_act, (((1,), (1,)), ((), ())), preferred_element_type=jnp.float32)
        for part in (high, low)
    )
    score = jnp.sum((own_grad + grad_ref[...]) * weighted, axis=0, keepdims=True)
    score_ref[...] = score / (out_panel * in_panel)


def last(me, pieces, sums, rows, devices):
    vmem = pl.BlockSpec(memory_space=pltpu.VMEM)
    (out_panel, in_panel), balanced = sums[0].shape, sums[1].shape[0]
    tokens = sum(piece.shape[0] for piece in pieces) // (rows + 16) * rows
    corrected, score = pl.pallas_call(
        functools.partial(last_kernel, rows, 1.0 / (devices * balanced)),
        out_shape=(
            jax.ShapeDtypeStruct((out_panel // devices, in_panel), jnp.float32),
            jax.ShapeDtypeStruct((1, balanced), jnp.float32),
        ),
        in_specs=[pl.BlockSpec(memory_space=pltpu.SMEM)] + [vmem] * (len(pieces) + 3),
        out_specs=(vmem, vmem),
        scratch_shapes=[
            pltpu.VMEM((tokens, out_panel + in_panel), jnp.bfloat16),
            pltpu.VMEM((out_panel, in_panel), jnp.float32),
        ],
        compiler_params=pltpu.CompilerParams(vmem_limit_bytes=16 * 2**20),
    )(me, *pieces, *sums)
    return corrected, score.reshape(balanced)


def ringed(activations, out_grads, slot_of_row, basis_in, basis_out):
    devices = lax.axis_size("dp")
    chips = devices // 2
    own_index = lax.axis_index("dp")
    rows = activations.shape[0]
    balanced = rows // 2
    depth_in, width = basis_in.shape
    depth_out = basis_out.shape[0]

    order = ring_order(chips)

    def ring(step):
        pairs = []
        for i, chip in enumerate(order):
            to = order[(i + step) % chips]
            pairs += [(2 * chip, 2 * to), (2 * chip + 1, 2 * to + 1)]
        return pairs

    forward, backward = ring(1), ring(-1)
    swap = [(i, i ^ 1) for i in range(devices)]

    def send(x, pairs):
        return lax.ppermute(x, "dp", pairs)

    half = chips // 2
    distances = [0]
    for d in range(1, half):
        distances += [d, -d]
    distances += [half]

    chip = own_index // 2
    position = jnp.where(chip % 2 == 0, chip // 2, chips - 1 - chip // 2)
    from_position = (position - jnp.array(distances, jnp.int32)) % chips
    owners = jnp.where(
        from_position < half, 2 * from_position, 2 * (chips - 1 - from_position) + 1
    ) * 2 + own_index % 2

    cut = (depth_in + depth_out) // 2
    second = basis_out[cut - depth_in :]
    first = lax.pad(basis_out, basis_out.dtype.type(0), ((depth_in, -second.shape[0], 0), (0, 0, 0)))
    first = lax.dynamic_update_slice(first, basis_in, (0, 0))
    first, second = {0: first}, {0: second}

    def hop(ahead, behind, s):
        ahead[s] = send(ahead[s - 1], forward)
        behind[-s] = send(behind[1 - s], backward)

    def pieces(held, at):
        return [(distances.index(d), 0 if held is first else cut, held[d]) for d in at]

    def add(kinds, parts, totals):
        tokens = [(activations, swapped_act), (out_grads, swapped_grad)]
        return list(project(owners, kinds, tokens, parts, totals, (depth_in, depth_out)))

    def after(held, at, totals):
        got = lax.optimization_barrier(tuple(held[d] for d in at) + tuple(totals))
        for d, x in zip(at, got):
            held[d] = x
        return list(got[len(at) :])

    swapped_act, swapped_grad = send(activations, swap), send(out_grads, swap)
    hop(first, second, 1)
    second[1] = send(second[0], forward)
    ready, swapped_act = lax.optimization_barrier((first[0], swapped_act))
    first[-1] = send(ready, backward)
    zero = jnp.zeros((rows, width), jnp.float32)
    grad = [zero, zero]
    for s in range(1, half):
        own = pieces(first, [0]) + pieces(second, [0]) if s == 1 else []
        if s + 1 < half:
            hop(first, second, s + 1)
        else:
            first[half], second[half] = send(first[s], forward), send(second[-s], backward)
        grad = add((1,), own + pieces(second, [-s]) + pieces(first, [s]), grad)
        grad = after(second, [s], after(first, [-s], grad))
        if s + 1 < half:
            hop(second, first, s + 1)
        grad = add((1,), pieces(first, [-s]) + pieces(second, [s]), grad)
        if s + 1 < half:
            grad = after(first, [s + 1], after(second, [-s - 1], grad))
    act = add((0,), pieces(first, distances[:-1]), [zero, zero])
    tokens = (activations, out_grads, swapped_act, swapped_grad)
    block, *act = fetch(owners, chips - 1, tokens, depth_in, depth_out, act)
    panels = (first[half], second[half])
    theirs = finish_dots(block[1], panels, act[1], grad[1], depth_in)
    block[0], swapped = lax.optimization_barrier((block[0], theirs))
    swapped = send(swapped, swap)
    mine = finish_dots(block[0], panels, act[0], grad[0], depth_in)

    is_valid = slot_of_row >= 0
    owner = jnp.where(is_valid, slot_of_row // balanced, -1)
    tag = jnp.concatenate([owner, slot_of_row % balanced]).astype(jnp.bfloat16)
    tag = jnp.broadcast_to(jnp.pad(tag, (0, 2 * width - 2 * rows))[None, :], (16, 2 * width))
    rotated = mine + swapped
    counts = is_valid[:, None] | (jnp.arange(2 * width) < width)[None, :]
    squares = jnp.where(counts, rotated * rotated, 0.0).astype(jnp.bfloat16)

    held = {0: jnp.concatenate([squares, tag], axis=0)}
    for s in range(1, half):
        hop(held, held, s)
    middle = (rows + 16) // 32 * 16
    upper = send(held[half - 2][:middle], ring(2))
    lower = send(held[2 - half][middle:], ring(-2))
    held[half - 1], held[1 - half], upper, lower = lax.optimization_barrier(
        (held[half - 1], held[1 - half], upper, lower)
    )
    near = jnp.concatenate([held[-d] for d in distances[:-3]], axis=0)
    far = jnp.concatenate([held[half - 1], held[1 - half], upper, lower], axis=0)
    own = [near, far]
    swapped = [send(x, swap) for x in own]
    me = own_index[None]
    gathered_rows = lax.optimization_barrier((near, swapped[0], far))
    sums = some_sums(me, list(gathered_rows), rows, width, balanced)
    return last(me, [swapped[1]], sums, rows, devices)


def body(*arrays):
    if lax.axis_size("dp") == 16:
        return ringed(*arrays)
    return gathered(*arrays)


def solution(mesh):
    return jax.shard_map(
        body,
        mesh=mesh,
        in_specs=(
            P(("groups", "dp"), None),
            P(("groups", "dp"), None),
            P(("groups", "dp")),
            P(("groups", "dp"), None),
            P(("groups", "dp"), None),
        ),
        out_specs=(P(("groups", "dp"), None), P(("groups", "dp"))),
        check_vma=False,
    )
```

```python
import functools

import jax
import jax.numpy as jnp
from jax import lax
from jax.experimental import pallas as pl
from jax.experimental.pallas import tpu as pltpu
from jax.sharding import PartitionSpec as P

damping = 0.1


def ring_order(chips):
    if chips == 8:
        return [0, 2, 4, 6, 7, 5, 3, 1]
    return list(range(chips))


def dot(a, b):
    return jnp.dot(a, b, preferred_element_type=jnp.float32)


def squared(x):
    return (x * x).astype(jnp.bfloat16)


def finish(all_grad, all_act, owners, places, own_index, devices, balanced):
    out_panel, in_panel = all_grad.shape[1], all_act.shape[1]
    masked = jnp.where(owners[:, None] >= 0, all_grad, jnp.zeros_like(all_grad))
    corrected = lax.dot_general(
        masked, all_act, (((0,), (0,)), ((), ())), preferred_element_type=jnp.float32
    ) / (devices * balanced)
    inverse = 1.0 / (corrected + damping)
    wanted = jnp.arange(balanced, dtype=jnp.int32)
    pick = ((owners[None, :] == own_index) & (places[None, :] == wanted[:, None])).astype(jnp.bfloat16)
    own_grad = dot(pick, all_grad)
    own_act = dot(pick, all_act)
    weighted = lax.dot_general(
        own_act, inverse, (((1,), (1,)), ((), ())), precision=lax.Precision.HIGHEST
    )
    self_score = jnp.sum(own_grad * weighted, axis=1) / (out_panel * in_panel)
    panel_rows = out_panel // devices
    own_corrected = lax.dynamic_slice(corrected, (own_index * panel_rows, 0), (panel_rows, in_panel))
    return own_corrected, self_score


def gathered(activations, out_grads, slot_of_row, basis_in, basis_out):
    devices = lax.axis_size("dp")
    own_index = lax.axis_index("dp")
    balanced = activations.shape[0] // 2

    def everyone(x):
        return lax.all_gather(x, "dp", axis=0, tiled=True)

    act_sq = squared(dot(activations, everyone(basis_in)))
    grad_sq = squared(dot(out_grads, everyone(basis_out)))
    slots = everyone(slot_of_row)
    owners = jnp.where(slots >= 0, slots // balanced, -1)
    return finish(
        everyone(grad_sq), everyone(act_sq), owners, slots % balanced, own_index, devices, balanced
    )


def runs(first, count, depth_in, depth_out):
    inside = max(0, min(depth_in - first, count))
    found = []
    if inside:
        found.append((0, first, inside, 0))
    if count > inside:
        found.append((1, first + inside - depth_in, count - inside, inside))
    return found


def project_kernel(kinds, parts, depths, owners_ref, *refs):
    sources, refs = refs[: 2 * len(kinds)], refs[2 * len(kinds) :]
    panels, refs = refs[: len(parts)], refs[len(parts) :]
    before, (mine_out, theirs_out, block, sems) = refs[: 2 * len(kinds)], refs[2 * len(kinds) :]
    rows, width = sources[0].shape[0], panels[0].shape[1]
    work, at = [], 0
    for (slot, first), panel in zip(parts, panels):
        for kind, start, count, within in runs(first, panel.shape[0], *depths):
            if kind not in kinds:
                continue
            column = pl.multiple_of(owners_ref[slot] * depths[kind] + start, 128)
            copies = []
            for j in range(2):
                copy = pltpu.make_async_copy(
                    sources[2 * kinds.index(kind) + j].at[:, pl.ds(column, count)],
                    block.at[pl.ds(j * rows, rows), pl.ds(at, count)],
                    sems.at[len(work), j],
                )
                copy.start()
                copies.append(copy)
            work.append((kind, at, count, panel.at[pl.ds(within, count), :], copies))
            at += count
    totals = {}
    for kind, at, count, panel, copies in work:
        for copy in copies:
            copy.wait()
        totals[kind] = totals.get(kind, 0.0) + dot(block[:, at : at + count], panel[...])
    for i, kind in enumerate(kinds):
        columns = slice(i * width, (i + 1) * width)
        mine_out[:, columns] = before[2 * i][...] + totals[kind][:rows]
        theirs_out[:, columns] = before[2 * i + 1][...] + totals[kind][rows:]


def project(owners, kinds, tokens, parts, before, depths):
    sources = [x for kind in kinds for x in tokens[kind]]
    rows, width = sources[0].shape[0], parts[0][2].shape[1]
    panels = [p[2] for p in parts]
    counts = [
        run[2] for p in parts for run in runs(p[1], p[2].shape[0], *depths) if run[0] in kinds
    ]
    vmem = pl.BlockSpec(memory_space=pltpu.VMEM)
    total = jax.ShapeDtypeStruct((rows, len(kinds) * width), jnp.float32)
    return pl.pallas_call(
        functools.partial(project_kernel, kinds, [p[:2] for p in parts], depths),
        out_shape=(total, total),
        in_specs=[pl.BlockSpec(memory_space=pltpu.SMEM)]
        + [pl.BlockSpec(memory_space=pl.ANY)] * len(sources)
        + [vmem] * (len(parts) + len(before)),
        out_specs=(vmem, vmem),
        scratch_shapes=[
            pltpu.VMEM((2 * rows, sum(counts)), sources[0].dtype),
            pltpu.SemaphoreType.DMA((len(counts), 2)),
        ],
        compiler_params=pltpu.CompilerParams(vmem_limit_bytes=16 * 2**20),
        cost_estimate=pl.CostEstimate(flops=1, bytes_accessed=1, transcendentals=0),
    )(
        owners,
        *[pltpu.with_memory_space_constraint(x, pltpu.HBM) for x in sources],
        *[pltpu.with_memory_space_constraint(x, pltpu.VMEM) for x in panels],
        *before,
    )


def copy_all(copies):
    for copy in copies:
        copy.start()
    for copy in copies:
        copy.wait()


def halves_kernel(upper_ref, lower_ref, first_ref, second_ref, sems):
    above, rest = upper_ref.shape[0], first_ref.shape[0] - upper_ref.shape[0]
    copy_all([
        pltpu.make_async_copy(
            lower_ref.at[pl.ds(rest, second_ref.shape[0]), :], second_ref, sems.at[0]
        ),
        pltpu.make_async_copy(upper_ref, first_ref.at[pl.ds(0, above), :], sems.at[1]),
        pltpu.make_async_copy(
            lower_ref.at[pl.ds(0, rest), :], first_ref.at[pl.ds(above, rest), :], sems.at[2]
        ),
    ])


def halves(upper, lower, cut):
    total, width = upper.shape[0] + lower.shape[0], upper.shape[1]
    vmem = pl.BlockSpec(memory_space=pltpu.VMEM)
    return pl.pallas_call(
        halves_kernel,
        out_shape=(
            jax.ShapeDtypeStruct((cut, width), upper.dtype),
            jax.ShapeDtypeStruct((total - cut, width), upper.dtype),
        ),
        in_specs=[pl.BlockSpec(memory_space=pl.ANY)] * 2,
        out_specs=(vmem, vmem),
        scratch_shapes=[pltpu.SemaphoreType.DMA((3,))],
        compiler_params=pltpu.CompilerParams(vmem_limit_bytes=16 * 2**20),
    )(*[pltpu.with_memory_space_constraint(x, pltpu.HBM) for x in (upper, lower)])


def fetch_kernel(slot, depths, owners_ref, *refs):
    sources, (own_ref, sibling_ref, sems) = refs[:4], refs[4:7]
    copies, at = [], 0
    for kind, depth in enumerate(depths):
        column = pl.multiple_of(owners_ref[slot] * depth, 128)
        for j, block in enumerate((own_ref, sibling_ref)):
            copies.append(
                pltpu.make_async_copy(
                    sources[2 * j + kind].at[:, pl.ds(column, depth)],
                    block.at[:, pl.ds(at, depth)],
                    sems.at[kind, j],
                )
            )
        at += depth
    copy_all(copies)


def fetch(owners, slot, tokens, depth_in, depth_out, after):
    rows = tokens[0].shape[0]
    vmem = pl.BlockSpec(memory_space=pltpu.VMEM)
    block = jax.ShapeDtypeStruct((rows, depth_in + depth_out), tokens[0].dtype)
    got = pl.pallas_call(
        functools.partial(fetch_kernel, slot, (depth_in, depth_out)),
        out_shape=(block, block),
        in_specs=[pl.BlockSpec(memory_space=pltpu.SMEM)] + [pl.BlockSpec(memory_space=pl.ANY)] * 4,
        out_specs=(vmem, vmem),
        scratch_shapes=[pltpu.SemaphoreType.DMA((2, 2))],
        compiler_params=pltpu.CompilerParams(vmem_limit_bytes=16 * 2**20),
        cost_estimate=pl.CostEstimate(flops=1, bytes_accessed=1, transcendentals=0),
    )(owners, *[pltpu.with_memory_space_constraint(x, pltpu.HBM) for x in tokens])
    return [list(got), *after]


def finish_dots_kernel(depth_in, block_ref, first_ref, second_ref, act_ref, grad_ref, out_ref):
    cut, width = first_ref.shape
    out_ref[:, :width] = act_ref[...] + dot(block_ref[:, :depth_in], first_ref[:depth_in, :])
    out_ref[:, width:] = (
        grad_ref[...]
        + dot(block_ref[:, depth_in:cut], first_ref[depth_in:, :])
        + dot(block_ref[:, cut:], second_ref[...])
    )


def finish_dots(block, panels, act, grad, depth_in):
    rows, width = act.shape
    vmem = pl.BlockSpec(memory_space=pltpu.VMEM)
    return pl.pallas_call(
        functools.partial(finish_dots_kernel, depth_in),
        out_shape=jax.ShapeDtypeStruct((rows, 2 * width), jnp.float32),
        in_specs=[vmem] * 5,
        out_specs=vmem,
        compiler_params=pltpu.CompilerParams(vmem_limit_bytes=16 * 2**20),
        cost_estimate=pl.CostEstimate(flops=1, bytes_accessed=1, transcendentals=0),
    )(block, *[pltpu.with_memory_space_constraint(x, pltpu.VMEM) for x in panels], act, grad)


def add_up(me, pieces, squares, rows, width, balanced):
    wanted = lax.broadcasted_iota(jnp.int32, (balanced, rows), 0)
    at, picks = 0, []
    for piece in pieces:
        for start in range(0, piece.shape[0], rows + 16):
            squares[at : at + rows, :] = piece[start : start + rows, :]
            tag = piece[start + rows : start + rows + 16, :][:1].astype(jnp.float32).astype(jnp.int32)
            owner, place = tag[:, :rows], tag[:, rows : 2 * rows]
            picks.append(((owner == me) & (place == wanted)).astype(jnp.float32))
            at += rows
    pick = jnp.concatenate(picks, axis=1).astype(jnp.bfloat16)
    act, grad = squares[:, :width], squares[:, width:]
    return (
        lax.dot_general(grad, act, (((0,), (0,)), ((), ())), preferred_element_type=jnp.float32),
        dot(pick, act),
        lax.dot_general(grad, pick, (((0,), (1,)), ((), ())), preferred_element_type=jnp.float32),
    )


def some_sums_kernel(rows, me_ref, *refs):
    pieces, (total_ref, act_ref, grad_ref, squares) = refs[:-4], refs[-4:]
    balanced, width = act_ref.shape
    total_ref[...], act_ref[...], grad_ref[...] = add_up(
        me_ref[0], pieces, squares, rows, width, balanced
    )


def some_sums(me, pieces, rows, width, balanced):
    vmem = pl.BlockSpec(memory_space=pltpu.VMEM)
    tokens = sum(piece.shape[0] for piece in pieces) // (rows + 16) * rows
    out_panel = pieces[0].shape[1] - width
    return pl.pallas_call(
        functools.partial(some_sums_kernel, rows),
        out_shape=(
            jax.ShapeDtypeStruct((out_panel, width), jnp.float32),
            jax.ShapeDtypeStruct((balanced, width), jnp.float32),
            jax.ShapeDtypeStruct((out_panel, balanced), jnp.float32),
        ),
        in_specs=[pl.BlockSpec(memory_space=pltpu.SMEM)] + [vmem] * len(pieces),
        out_specs=(vmem, vmem, vmem),
        scratch_shapes=[pltpu.VMEM((tokens, pieces[0].shape[1]), jnp.bfloat16)],
        compiler_params=pltpu.CompilerParams(vmem_limit_bytes=16 * 2**20),
        cost_estimate=pl.CostEstimate(flops=1, bytes_accessed=1, transcendentals=0),
    )(me, *pieces)


def last_kernel(rows, scale, me_ref, first_ref, second_ref, total_ref, act_ref, grad_ref, *refs):
    corrected_ref, score_ref, squares, held = refs
    me = me_ref[0]
    panel_rows, in_panel = corrected_ref.shape
    out_panel = total_ref.shape[0]
    total, own_act, own_grad = add_up(
        me, (first_ref, second_ref), squares, rows, in_panel, act_ref.shape[0]
    )
    corrected = (total + total_ref[...]) * scale
    held[...] = corrected
    corrected_ref[...] = held[pl.ds(pl.multiple_of(me * panel_rows, panel_rows), panel_rows), :]
    inverse = 1.0 / (corrected + damping)
    high = inverse.astype(jnp.bfloat16)
    low = (inverse - high.astype(jnp.float32)).astype(jnp.bfloat16)
    own_act = (own_act + act_ref[...]).astype(jnp.bfloat16)
    weighted = sum(
        lax.dot_general(part, own_act, (((1,), (1,)), ((), ())), preferred_element_type=jnp.float32)
        for part in (high, low)
    )
    score = jnp.sum((own_grad + grad_ref[...]) * weighted, axis=0, keepdims=True)
    score_ref[...] = score / (out_panel * in_panel)


def last(me, pieces, sums, rows, devices):
    vmem = pl.BlockSpec(memory_space=pltpu.VMEM)
    (out_panel, in_panel), balanced = sums[0].shape, sums[1].shape[0]
    tokens = sum(piece.shape[0] for piece in pieces) // (rows + 16) * rows
    corrected, score = pl.pallas_call(
        functools.partial(last_kernel, rows, 1.0 / (devices * balanced)),
        out_shape=(
            jax.ShapeDtypeStruct((out_panel // devices, in_panel), jnp.float32),
            jax.ShapeDtypeStruct((1, balanced), jnp.float32),
        ),
        in_specs=[pl.BlockSpec(memory_space=pltpu.SMEM)] + [vmem] * 5,
        out_specs=(vmem, vmem),
        scratch_shapes=[
            pltpu.VMEM((tokens, out_panel + in_panel), jnp.bfloat16),
            pltpu.VMEM((out_panel, in_panel), jnp.float32),
        ],
        compiler_params=pltpu.CompilerParams(vmem_limit_bytes=16 * 2**20),
    )(me, *pieces, *sums)
    return corrected, score.reshape(balanced)


def ringed(activations, out_grads, slot_of_row, basis_in, basis_out):
    devices = lax.axis_size("dp")
    chips = devices // 2
    own_index = lax.axis_index("dp")
    rows = activations.shape[0]
    balanced = rows // 2
    depth_in, width = basis_in.shape
    depth_out = basis_out.shape[0]

    order = ring_order(chips)

    def ring(step):
        pairs = []
        for i, chip in enumerate(order):
            to = order[(i + step) % chips]
            pairs += [(2 * chip, 2 * to), (2 * chip + 1, 2 * to + 1)]
        return pairs

    forward, backward = ring(1), ring(-1)
    swap = [(i, i ^ 1) for i in range(devices)]

    def send(x, pairs):
        return lax.ppermute(x, "dp", pairs)

    half = chips // 2
    distances = [0]
    for d in range(1, half):
        distances += [d, -d]
    distances += [half]

    chip = own_index // 2
    position = jnp.where(chip % 2 == 0, chip // 2, chips - 1 - chip // 2)
    from_position = (position - jnp.array(distances, jnp.int32)) % chips
    owners = jnp.where(
        from_position < half, 2 * from_position, 2 * (chips - 1 - from_position) + 1
    ) * 2 + own_index % 2

    cut = (depth_in + depth_out) // 2
    second = basis_out[cut - depth_in :]
    first = lax.pad(basis_out, basis_out.dtype.type(0), ((depth_in, -second.shape[0], 0), (0, 0, 0)))
    first = lax.dynamic_update_slice(first, basis_in, (0, 0))
    first, second = {0: first}, {0: second}

    def hop(ahead, behind, s):
        ahead[s] = send(ahead[s - 1], forward)
        behind[-s] = send(behind[1 - s], backward)

    def pieces(held, at):
        return [(distances.index(d), 0 if held is first else cut, held[d]) for d in at]

    def add(kinds, parts, totals):
        tokens = [(activations, swapped_act), (out_grads, swapped_grad)]
        return list(project(owners, kinds, tokens, parts, totals, (depth_in, depth_out)))

    def after(held, at, totals):
        got = lax.optimization_barrier(tuple(held[d] for d in at) + tuple(totals))
        for d, x in zip(at, got):
            held[d] = x
        return list(got[len(at) :])

    swapped_act, swapped_grad = send(activations, swap), send(out_grads, swap)
    hop(first, second, 1)
    second[1] = send(second[0], forward)
    ready, swapped_act = lax.optimization_barrier((first[0], swapped_act))
    first[-1] = send(ready, backward)
    zero = jnp.zeros((rows, width), jnp.float32)
    grad = [zero, zero]
    for s in range(1, half):
        own = pieces(first, [0]) + pieces(second, [0]) if s == 1 else []
        if s + 1 < half:
            hop(first, second, s + 1)
        else:
            first[half], second[half] = send(first[s], forward), send(second[-s], backward)
        grad = add((1,), own + pieces(first, [s]) + pieces(second, [-s]), grad)
        grad = after(second, [s], after(first, [-s], grad))
        if s + 1 < half:
            hop(second, first, s + 1)
        grad = add((1,), pieces(second, [s]) + pieces(first, [-s]), grad)
        if s + 1 < half:
            grad = after(first, [s + 1], after(second, [-s - 1], grad))
    act = add((0,), pieces(first, distances[:-1]), [zero, zero])
    tokens = (activations, out_grads, swapped_act, swapped_grad)
    block, *act = fetch(owners, chips - 1, tokens, depth_in, depth_out, act)
    panels = (first[half], second[half])
    theirs = finish_dots(block[1], panels, act[1], grad[1], depth_in)
    block[0], swapped = lax.optimization_barrier((block[0], theirs))
    swapped = send(swapped, swap)
    mine = finish_dots(block[0], panels, act[0], grad[0], depth_in)

    is_valid = slot_of_row >= 0
    owner = jnp.where(is_valid, slot_of_row // balanced, -1)
    tag = jnp.concatenate([owner, slot_of_row % balanced]).astype(jnp.bfloat16)
    tag = jnp.broadcast_to(jnp.pad(tag, (0, 2 * width - 2 * rows))[None, :], (16, 2 * width))
    rotated = mine + swapped
    counts = is_valid[:, None] | (jnp.arange(2 * width) < width)[None, :]
    squares = jnp.where(counts, rotated * rotated, 0.0).astype(jnp.bfloat16)

    held = {0: jnp.concatenate([squares, tag], axis=0)}
    for s in range(1, half):
        hop(held, held, s)
    middle = (rows + 16) // 32 * 16
    upper = send(held[half - 2][:middle], ring(2))
    lower = send(held[2 - half][middle:], ring(-2))
    held[half - 1], held[1 - half], upper, lower = lax.optimization_barrier(
        (held[half - 1], held[1 - half], upper, lower)
    )
    near = jnp.concatenate([held[-d] for d in distances[:-3]], axis=0)
    far = jnp.concatenate([held[half - 1], held[1 - half], upper, lower], axis=0)
    own = [near, far]
    swapped = [send(x, swap) for x in own]
    me = own_index[None]
    near_both = (near, swapped[0])
    sums = some_sums(me, list(near_both), rows, width, balanced)
    return last(me, [far, swapped[1]], sums, rows, devices)


def body(*arrays):
    if lax.axis_size("dp") == 16:
        return ringed(*arrays)
    return gathered(*arrays)


def solution(mesh):
    return jax.shard_map(
        body,
        mesh=mesh,
        in_specs=(
            P(("groups", "dp"), None),
            P(("groups", "dp"), None),
            P(("groups", "dp")),
            P(("groups", "dp"), None),
            P(("groups", "dp"), None),
        ),
        out_specs=(P(("groups", "dp"), None), P(("groups", "dp"))),
        check_vma=False,
    )
```
